32 devices in a mesh: leaf: 4 (over z), row: 4 (over y, core), col: 2 (over x).
Axes of the slice: x: 2, y: 2, z: 4, core: 2. Of those that a mesh axis runs over, the one named last changes fastest.
Arguments:
- child_loads: bfloat16 [8, 128, 6144], P('leaf', None, 'row'), may hold values from -6 to 6
- child_inverse: bfloat16 [8, 6144, 6144], P('leaf', 'row', 'col'), as said below
- child_panel: bfloat16 [8, 6144, 6144], P('leaf', 'row', 'col'), may hold values from -0.0390625 to 0.0390625
- child_map: int32 [8, 6144], P('leaf'), may hold values from 0 to 6144, as said below
- root_loads: bfloat16 [128, 6144], P(None, 'row'), may hold values from -6 to 6
- root_inverse: bfloat16 [6144, 6144], P('row', 'col'), as said below
Outputs:
- child_solution: float32 [8, 128, 6144], P('leaf', None, 'row')
- root_solution: float32 [128, 6144], P(None, 'row')
The draws below stay inside these ranges and needn't reach their ends.
Inputs may be any that keep to these rules, and one draw needn't show every extreme that they name: `child_map`: entry [k, j] is the root-front row into which update slot j of child front k adds, or 6144 where the slot is padding. Within each aligned block of 128 slots the live slots come first; the first block of every child is full; the live rows of one child are distinct. `child_inverse`: each child's [6144, 6144] block is upper triangular with a positive diagonal. `root_inverse`: upper triangular with a positive diagonal.
All inputs are finite; a program needn't handle non-finite values.
Results may differ from the reference program's by a relative error of at most 0.025.
Values may be sent and summed in bfloat16 or wider, within the bound.
No kernel may reach another device: no remote copies, remote signals or barrier semaphores. Data moves between devices by JAX's collectives and lax.ppermute only.
A program may use at most 128 MiB of HBM per device.

```python
import math
import jax
import jax.numpy as jnp
from jax import lax

S = 6144
U = 6144
P_SIZE = 6144
NRHS = 128
KIDS = 8


def upper_factor(key, count, order):
    key_off, key_diag = jax.random.split(key)
    off_terms = jax.random.normal(key_off, (count, order, order), jnp.float32)
    diag_terms = jnp.exp(jax.random.uniform(key_diag, (count, 1, order), jnp.float32, math.log(0.5), math.log(2.0)))
    row_ids = lax.broadcasted_iota(jnp.int32, (count, order, order), 1)
    col_ids = lax.broadcasted_iota(jnp.int32, (count, order, order), 2)
    scaled = off_terms * (0.7 / math.sqrt(order))
    return jnp.where(col_ids > row_ids, scaled, jnp.where(col_ids == row_ids, diag_terms, 0.0))


def draw_child_inverse(key, part):
    return upper_factor(jax.random.fold_in(key, 3), KIDS, S).astype(jnp.bfloat16)


def draw_root_inverse(key, part):
    return upper_factor(jax.random.fold_in(key, 11), 1, P_SIZE)[0].astype(jnp.bfloat16)


def one_child_map(child_key):
    key_rows, key_count = jax.random.split(child_key)
    chosen = jax.random.permutation(key_rows, P_SIZE)[:U]
    live_count = jax.random.randint(key_count, (U // 128,), 32, 129)
    live_count = live_count.at[0].set(128)
    slot_pos = jnp.arange(U) % 128
    block_id = jnp.arange(U) // 128
    return jnp.where(slot_pos < live_count[block_id], chosen, P_SIZE).astype(jnp.int32)


def draw_child_map(key, part):
    child_keys = jax.random.split(jax.random.fold_in(key, 7), KIDS)
    return jax.vmap(one_child_map)(child_keys)


def levels(key, extent, shards, least, top_value):
    level = 1.0
    for axis_at, blocks in shards:
        steps = jax.random.uniform(jax.random.fold_in(jax.random.fold_in(key, 6), axis_at), (blocks,), jnp.float32, least / len(shards), top_value / len(shards))
        level = level * jnp.repeat(jnp.exp(steps), extent[axis_at] // blocks).reshape((-1,) + (1,) * (len(extent) - 1 - axis_at))
    return level


def bell_draw(rng, extent, spread, bound, cuts=(), held_as=jnp.bfloat16):
    factor_of = levels(rng, extent, cuts, -0.22, 0.18) if cuts else 1.0
    drawn = jax.random.normal(rng, extent, jnp.float32) * spread * factor_of
    return jnp.minimum(jnp.maximum(drawn, -bound), bound).astype(held_as)


def setup_inputs(seed: int = 0) -> dict:
    key_of = jax.random.split(jax.random.key(seed), 7)
    return {
        "child_loads": bell_draw(key_of[0], (KIDS, NRHS, S), 1.0, 6.0, ((0, 4), (2, 4))),
        "child_inverse": draw_child_inverse(jax.random.fold_in(key_of[6], 71), 0),
        "child_panel": bell_draw(key_of[2], (KIDS, U, S), (4 * S) ** -0.5, 0.0390625, ((0, 4), (1, 4), (2, 2))),
        "child_map": draw_child_map(jax.random.fold_in(key_of[6], 71), 0),
        "root_loads": bell_draw(key_of[4], (NRHS, P_SIZE), 1.0, 6.0, ((1, 4),)),
        "root_inverse": draw_root_inverse(jax.random.fold_in(key_of[6], 71), 0),
    }


def product(left, right):
    return jnp.dot(left.astype(jnp.float32), right.astype(jnp.float32), preferred_element_type=jnp.float32, precision=lax.Precision.HIGHEST)


def child_forward(pieces):
    load_rows, inverse, panel_rows = pieces
    forward_solved = product(load_rows, inverse)
    update_vals = product(forward_solved.astype(jnp.bfloat16), panel_rows.T)
    return forward_solved, update_vals.astype(jnp.bfloat16)


def reference(child_loads, child_inverse, child_panel, child_map, root_loads, root_inverse):
    forward_solved, update_vals = lax.map(child_forward, (child_loads, child_inverse, child_panel))
    values = jnp.transpose(update_vals, (1, 0, 2)).reshape(NRHS, KIDS * U).astype(jnp.float32)
    target = child_map.reshape(-1).astype(jnp.int32)
    extended = jnp.zeros((NRHS, P_SIZE + 1), jnp.float32).at[:, target].add(values)[:, :P_SIZE]
    residual = root_loads.astype(jnp.float32) - extended
    root_forward = product(residual.astype(jnp.bfloat16), root_inverse)
    root_solution = product(root_forward.astype(jnp.bfloat16), root_inverse.T)
    padded_root = jnp.concatenate([root_solution.astype(jnp.bfloat16), jnp.zeros((NRHS, 1), jnp.bfloat16)], axis=1)

    def child_backward(pieces):
        forward_one, panel_rows, map_rows, inverse = pieces
        picked = jnp.take(padded_root, map_rows.astype(jnp.int32), axis=1)
        remainder = forward_one - product(picked, panel_rows)
        return product(remainder.astype(jnp.bfloat16), inverse.T)

    child_solution = lax.map(child_backward, (forward_solved, child_panel, child_map, child_inverse))
    return child_solution, root_solution
```

```python
import functools

import jax
import jax.numpy as jnp
from jax import lax
from jax.experimental import pallas as pl
from jax.experimental.pallas import tpu as pltpu
from jax.sharding import PartitionSpec as P

BF16 = jnp.bfloat16
F32 = jnp.float32
NN = (((1,), (0,)), ((), ()))
NT = (((1,), (1,)), ((), ()))


def tile_of(extent, *sizes):
    for size in sizes:
        if extent % size == 0:
            return size
    return extent


def params():
    return pltpu.CompilerParams(vmem_limit_bytes=40 * 1024 * 1024)


def cost(flops, nbytes):
    return pl.CostEstimate(flops=flops, bytes_accessed=nbytes, transcendentals=0)


def nn_kernel(half_ref, x_ref, w_ref, o_ref):
    o_ref[...] = lax.dot_general(
        x_ref[...], w_ref[0], NN, preferred_element_type=F32
    ).astype(o_ref.dtype)


def nn_half(x, w, child, half, dtype):
    m, k = x.shape
    n_half = w.shape[2] // 2
    bn = tile_of(n_half, 512, 384, 256, 128)
    steps = n_half // bn
    return pl.pallas_call(
        nn_kernel,
        grid_spec=pltpu.PrefetchScalarGridSpec(
            num_scalar_prefetch=1,
            grid=(steps,),
            in_specs=[
                pl.BlockSpec((m, k), lambda i, h: (0, 0)),
                pl.BlockSpec((1, k, bn), lambda i, h: (child, 0, h[0] * steps + i)),
            ],
            out_specs=pl.BlockSpec((m, bn), lambda i, h: (0, i)),
        ),
        out_shape=jax.ShapeDtypeStruct((m, n_half), dtype),
        compiler_params=params(),
        cost_estimate=cost(2 * m * k * n_half, 2 * k * n_half),
    )(half, x, w)


def nt_kernel(half_ref, a_ref, b_ref, wa_ref, wb_ref, o_ref):
    total = lax.dot_general(a_ref[...], wa_ref[0], NT, preferred_element_type=F32)
    total += lax.dot_general(b_ref[...], wb_ref[0], NT, preferred_element_type=F32)
    o_ref[...] = total.astype(o_ref.dtype)


def nt(mine, other, w, child, half, dtype):
    m, k_half = mine.shape
    u = w.shape[1]
    bu = tile_of(u, 256, 128)
    return pl.pallas_call(
        nt_kernel,
        grid_spec=pltpu.PrefetchScalarGridSpec(
            num_scalar_prefetch=1,
            grid=(u // bu,),
            in_specs=[
                pl.BlockSpec((m, k_half), lambda i, h: (0, 0)),
                pl.BlockSpec((m, k_half), lambda i, h: (0, 0)),
                pl.BlockSpec((1, bu, k_half), lambda i, h: (child, i, h[0])),
                pl.BlockSpec((1, bu, k_half), lambda i, h: (child, i, 1 - h[0])),
            ],
            out_specs=pl.BlockSpec((m, bu), lambda i, h: (0, i)),
        ),
        out_shape=jax.ShapeDtypeStruct((m, u), dtype),
        compiler_params=params(),
        cost_estimate=cost(4 * m * k_half * u, 4 * k_half * u),
    )(half, mine, other, w, w)


def one_hot(rows, first_row, slot_map):
    local = (slot_map - first_row).astype(jnp.int16)
    row_ids = lax.broadcasted_iota(jnp.int16, (rows, slot_map.shape[1]), 0)
    return jnp.where(row_ids == local, BF16(1), BF16(0))


def scatter_kernel(block_rows, tile, odd, *refs):
    row_ref, map_ref, upd_ref, *rest = refs
    o_ref = rest[-1]
    j, t = pl.program_id(0), pl.program_id(1)
    dest = lax.bitwise_xor(row_ref[0], 2 * j + odd)
    hot = one_hot(tile, dest * block_rows + t * tile, map_ref[...])
    total = lax.dot_general(upd_ref[...], hot, NT, preferred_element_type=F32)
    if len(rest) == 2:
        total += rest[0][0].astype(F32)
    o_ref[0] = total.astype(o_ref.dtype)


def scatter(upd, slot_map, row, rows_count, block_rows, odd, before):
    m, u = upd.shape
    tile = tile_of(block_rows, 256, 128)
    count = rows_count // 2
    in_specs = [
        pl.BlockSpec((1, u), lambda j, t, r: (0, 0)),
        pl.BlockSpec((m, u), lambda j, t, r: (0, 0)),
    ]
    block = pl.BlockSpec((1, m, tile), lambda j, t, r: (j, 0, t))
    args = [slot_map, upd]
    if before is not None:
        in_specs.append(block)
        args.append(before)
    return pl.pallas_call(
        functools.partial(scatter_kernel, block_rows, tile, odd),
        grid_spec=pltpu.PrefetchScalarGridSpec(
            num_scalar_prefetch=1,
            grid=(count, block_rows // tile),
            in_specs=in_specs,
            out_specs=block,
        ),
        out_shape=jax.ShapeDtypeStruct((count, m, block_rows), BF16),
        compiler_params=params(),
        cost_estimate=cost(2 * m * u * count * block_rows, 4 * m * count * block_rows),
    )(row, *args)


def gather_kernel(block_rows, tile, rows_at, *refs):
    row_ref, map_ref, root_ref, *rest = refs
    o_ref = rest[-1]
    slot_map = map_ref[0]
    total = None
    for at, (array, which) in enumerate(rows_at):
        first = lax.bitwise_xor(row_ref[0], which) * block_rows
        for start in range(0, block_rows, tile):
            hot = one_hot(tile, first + start, slot_map)
            term = lax.dot_general(
                root_ref[at, :, start : start + tile], hot, NN, preferred_element_type=F32
            )
            total = term if total is None else total + term
    if len(rest) == 2:
        total += rest[0][...].astype(F32)
    o_ref[...] = total.astype(o_ref.dtype)


def gather(root, which, slot_map, row, before):
    blocks, m, block_rows = root.shape
    u = slot_map.shape[2]
    tile = tile_of(block_rows, 512, 384, 256, 128)
    bu = tile_of(u, 512, 384, 256, 128)
    in_specs = [
        pl.BlockSpec((1, 1, bu), lambda i, r: (0, 0, i)),
        pl.BlockSpec((blocks, m, block_rows), lambda i, r: (0, 0, 0)),
    ]
    out_block = pl.BlockSpec((m, bu), lambda i, r: (0, i))
    args = [slot_map, root]
    if before is not None:
        in_specs.append(out_block)
        args.append(before)
    return pl.pallas_call(
        functools.partial(
            gather_kernel, block_rows, tile, [(0, x) for x in which]
        ),
        grid_spec=pltpu.PrefetchScalarGridSpec(
            num_scalar_prefetch=1, grid=(u // bu,), in_specs=in_specs, out_specs=out_block
        ),
        out_shape=jax.ShapeDtypeStruct((m, u), BF16),
        compiler_params=params(),
        cost_estimate=cost(2 * m * u * blocks * block_rows, 2 * m * blocks * block_rows),
    )(row, *args)


def swap(x, axis, bit, size):
    return lax.ppermute(x, axis, [(i, i ^ bit) for i in range(size)])


def bits(size):
    return [1 << b for b in range(size.bit_length() - 1)]


def on_device(sizes, child_loads, child_inverse, child_panel, child_map, root_loads, root_inverse):
    leafs, rows, cols = sizes
    kids = child_loads.shape[0]
    case_count, root_rows = root_loads.shape
    leaf, row, col = (lax.axis_index(a).astype(jnp.int32) for a in ("leaf", "row", "col"))
    core = lax.bitwise_and(row, 1)
    mine = core[None]
    other = (1 - core)[None]
    row_1 = row[None]
    root_w = root_inverse[None]

    def row_sum(x, w, child):
        sent = nn_half(x, w, child, other, BF16)
        kept = nn_half(x, w, child, mine, F32)
        total = kept + swap(sent, "row", 1, rows).astype(F32)
        for bit in bits(rows)[1:]:
            total = total + swap(total.astype(BF16), "row", bit, rows).astype(F32)
        return total

    def times_transposed(half_cols, w, child):
        rounded = half_cols.astype(BF16)
        return nt(rounded, swap(rounded, "row", 1, rows), w, child, mine, BF16)

    slot_rows = child_panel.shape[1]
    own_map = lax.dynamic_slice_in_dim(child_map, row * slot_rows, slot_rows, 1)
    maps = own_map.reshape(kids, 1, slot_rows)

    forward = [row_sum(child_loads[k], child_inverse, k) for k in range(kids)]
    sent = kept = None
    for k in range(kids):
        upd = times_transposed(forward[k], child_panel, k)
        sent = scatter(upd, maps[k], row_1, rows, root_rows, 1, sent)
        kept = scatter(upd, maps[k], row_1, rows, root_rows, 0, kept)

    total = kept.astype(F32) + swap(sent, "row", 1, rows).astype(F32)
    for bit in bits(rows)[1:]:
        away = total[1::2].astype(BF16)
        total = total[0::2] + swap(away, "row", bit, rows).astype(F32)
    total = total[0]
    chunk = case_count // leafs

    def cases_of(x, j):
        return lax.dynamic_slice_in_dim(x, lax.bitwise_xor(leaf, j) * chunk, chunk, 0)

    narrow = total.astype(BF16)
    mine_cases = cases_of(total, 0)
    for j in range(1, leafs):
        mine_cases = mine_cases + swap(cases_of(narrow, j), "leaf", j, leafs).astype(F32)
    for bit in bits(cols):
        narrow = mine_cases.astype(BF16)
        mine_cases = narrow.astype(F32) + swap(narrow, "col", bit, cols).astype(F32)
    residual = (cases_of(root_loads, 0).astype(F32) - mine_cases).astype(BF16)

    root_forward = row_sum(residual, root_w, 0)
    part = times_transposed(root_forward, root_w, 0)
    for bit in bits(cols):
        part = (part.astype(F32) + swap(part, "col", bit, cols).astype(F32)).astype(BF16)

    pieces = [part] + [swap(part, "leaf", j, leafs) for j in range(1, leafs)]
    own = jnp.zeros((case_count, root_rows), BF16)
    for j in range(leafs):
        own = lax.dynamic_update_slice_in_dim(own, pieces[j], lax.bitwise_xor(leaf, j) * chunk, 0)
    root_solution = own.astype(F32)

    groups = own[None]
    for bit in bits(rows)[1:]:
        groups = jnp.concatenate([groups, swap(groups, "row", bit, rows)])
    near = groups[:1]
    near_other = swap(near, "row", 1, rows)
    far = groups[1:]
    far_other = swap(far, "row", 1, rows)
    near_all = jnp.concatenate([near, near_other])
    far_all = jnp.concatenate([far, far_other])
    near_at = [0, 1]
    far_at = [2 * i for i in range(1, rows // 2)] + [2 * i + 1 for i in range(1, rows // 2)]

    solved = []
    picked = [gather(near_all, near_at, maps[k][None], row_1, None) for k in range(kids)]
    for k in range(kids):
        full = gather(far_all, far_at, maps[k][None], row_1, picked[k])
        back = row_sum(full, child_panel, k)
        rest = forward[k] - back
        out = times_transposed(rest, child_inverse, k)
        for bit in bits(cols):
            out = out.astype(F32) + swap(out.astype(BF16), "col", bit, cols).astype(F32)
            if bit != bits(cols)[-1]:
                out = out.astype(BF16)
        solved.append(out)
    return (jnp.stack(solved), root_solution)


def solution(mesh):
    sizes = tuple(mesh.shape[a] for a in ("leaf", "row", "col"))
    in_specs = (
        P("leaf", None, "row"),
        P("leaf", "row", "col"),
        P("leaf", "row", "col"),
        P("leaf", None),
        P(None, "row"),
        P("row", "col"),
    )
    out_specs = (P("leaf", None, "row"), P(None, "row"))
    return jax.shard_map(
        functools.partial(on_device, sizes),
        mesh=mesh,
        in_specs=in_specs,
        out_specs=out_specs,
        check_vma=False,
    )
```

```python
import functools

import jax
import jax.numpy as jnp
from jax import lax
from jax.experimental import pallas as pl
from jax.experimental.pallas import tpu as pltpu
from jax.sharding import PartitionSpec as P

BF16 = jnp.bfloat16
F32 = jnp.float32
I16 = jnp.int16
NN = (((1,), (0,)), ((), ()))
NT = (((1,), (1,)), ((), ()))
LANES = 128
ANY = pl.BlockSpec(memory_space=pl.ANY)


def tile_of(extent, *sizes):
    for size in sizes:
        if extent % size == 0:
            return size
    return extent


def params():
    return pltpu.CompilerParams(vmem_limit_bytes=20 * 1024 * 1024)


def cost(flops, nbytes):
    return pl.CostEstimate(flops=flops // 64, bytes_accessed=nbytes // 64, transcendentals=0)


def in_hbm(w):
    return pltpu.with_memory_space_constraint(w, pltpu.HBM)


def nn_kernel(steps, parts, half_ref, x_ref, w_ref, *rest):
    outs = rest[-len(parts):]
    x = x_ref[0] if len(x_ref.shape) == 3 else x_ref[...]
    product = lax.dot_general(x, w_ref[0], NN, preferred_element_type=F32)
    if len(parts) == 1:
        outs[0][...] = product.astype(outs[0].dtype)
        return
    for at, out in enumerate(outs):

        @pl.when(pl.program_id(0) // steps == at)
        def _(out=out):
            out[...] = product.astype(out.dtype)


def nn(x, w, child, core, parts, after=()):
    m, k = x.shape[-2:]
    n_half = w.shape[2] // 2
    bn = tile_of(n_half, 768, 512, 384, 256, 128)
    steps = n_half // bn
    count = len(parts)

    def w_at(i, h):
        part = i // steps
        which = (parts[0] + part * (parts[-1] - parts[0])) if count == 2 else parts[0]
        return (child, 0, lax.bitwise_xor(h[0], which) * steps + lax.rem(i, steps))

    def out_at(at):
        return lambda i, h: (0, jnp.clip(i - at * steps, 0, steps - 1))

    if x.ndim == 3:
        x_spec = pl.BlockSpec((1, m, k), lambda i, h: (child, 0, 0))
    else:
        x_spec = pl.BlockSpec((m, k), lambda i, h: (0, 0))
    outs = pl.pallas_call(
        functools.partial(nn_kernel, steps, parts),
        grid_spec=pltpu.PrefetchScalarGridSpec(
            num_scalar_prefetch=1,
            grid=(count * steps,),
            in_specs=[x_spec, pl.BlockSpec((1, k, bn), w_at)] + [ANY] * len(after),
            out_specs=[pl.BlockSpec((m, bn), out_at(at)) for at in range(count)],
        ),
        out_shape=[jax.ShapeDtypeStruct((m, n_half), BF16 if p else F32) for p in parts],
        compiler_params=params(),
        cost_estimate=cost(2 * m * k * n_half * count, 2 * k * n_half * count),
    )(core, x, in_hbm(w), *after)
    return outs


def nt_kernel(half_ref, a_ref, b_ref, wa_ref, wb_ref, *rest):
    o_ref = rest[-1]
    total = lax.dot_general(a_ref[...], wa_ref[0], NT, preferred_element_type=F32)
    total += lax.dot_general(b_ref[...], wb_ref[0], NT, preferred_element_type=F32)
    o_ref[...] = total.astype(o_ref.dtype)


def nt(mine, other, w, child, core, chunk=0, chunks=1, after=()):
    m, k_half = mine.shape
    u = w.shape[1] // chunks
    bu = tile_of(u, 512, 384, 256, 128)
    first = chunk * (u // bu)
    return pl.pallas_call(
        nt_kernel,
        grid_spec=pltpu.PrefetchScalarGridSpec(
            num_scalar_prefetch=1,
            grid=(u // bu,),
            in_specs=[
                pl.BlockSpec((m, k_half), lambda i, h: (0, 0)),
                pl.BlockSpec((m, k_half), lambda i, h: (0, 0)),
                pl.BlockSpec((1, bu, k_half), lambda i, h: (child, first + i, h[0])),
                pl.BlockSpec((1, bu, k_half), lambda i, h: (child, first + i, 1 - h[0])),
            ]
            + [ANY] * len(after),
            out_specs=pl.BlockSpec((m, bu), lambda i, h: (0, i)),
        ),
        out_shape=jax.ShapeDtypeStruct((m, u), BF16),
        compiler_params=params(),
        cost_estimate=cost(4 * m * k_half * u, 4 * k_half * u),
    )(core, mine, other, in_hbm(w), in_hbm(w), *after)


def spread_kernel(map_ref, o_ref):
    u = map_ref.shape[2]
    step = tile_of(u, LANES)
    for start in range(0, u, step):
        row = map_ref[0, :, start : start + step]
        o_ref[0, start : start + step, :] = jnp.broadcast_to(row, (LANES, step)).T.astype(I16)


def spread(maps):
    kids, _, u = maps.shape
    return pl.pallas_call(
        spread_kernel,
        grid=(kids,),
        in_specs=[pl.BlockSpec((1, 1, u), lambda k: (k, 0, 0))],
        out_specs=pl.BlockSpec((1, u, LANES), lambda k: (k, 0, 0)),
        out_shape=jax.ShapeDtypeStruct((kids, u, LANES), I16),
        compiler_params=params(),
        cost_estimate=cost(kids * u * LANES, 2 * kids * u * LANES),
    )(maps)


def store_in_order(order_ref, chunk, store, value):
    for i in range(value.shape[0] // chunk):
        store(
            pl.ds(pl.multiple_of(order_ref[i] * chunk, chunk), chunk),
            value[i * chunk : (i + 1) * chunk],
        )


def scatter_kernel(block_rows, tile, odd, chunk, *refs):
    row_ref, order_ref, map_ref, upd_ref, *rest = refs
    o_ref = rest[-1]
    j, t = pl.program_id(0), pl.program_id(1)
    dest = lax.bitwise_xor(row_ref[0], 2 * j + odd)
    first = (dest * block_rows + t * tile).astype(I16)
    local = map_ref[0] - first
    u = local.shape[0]
    sub = tile_of(tile, 256, 128)
    upd = upd_ref[...]
    for start in range(0, tile, sub):
        wide = jnp.concatenate([local] * (sub // LANES), axis=1)
        row_ids = lax.broadcasted_iota(I16, (u, sub), 1) + jnp.int16(start)
        hot = jnp.where(row_ids == wide, BF16(1), BF16(0))
        total = lax.dot_general(upd, hot, NN, preferred_element_type=F32)
        if len(rest) == 2:
            at = slice(start, start + sub)
            before = rest[0]

            def store(ds, value, at=at, before=before):
                o_ref[0, ds, at] = (value + before[0, ds, at].astype(F32)).astype(o_ref.dtype)

        else:
            at = slice(start, start + sub)

            def store(ds, value, at=at):
                o_ref[0, ds, at] = value.astype(o_ref.dtype)

        store_in_order(order_ref, chunk, store, total)


def scatter(upd, spread_maps, child, row, order, rows_count, block_rows, odd, before):
    m, u = upd.shape
    tile = tile_of(block_rows, 768, 512, 384, 256, 128)
    count = rows_count // 2
    chunk = m // order.shape[0]
    block = pl.BlockSpec((1, m, tile), lambda j, t, r, o: (j, 0, t))
    in_specs = [
        pl.BlockSpec((1, u, LANES), lambda j, t, r, o: (child, 0, 0)),
        pl.BlockSpec((m, u), lambda j, t, r, o: (0, 0)),
    ]
    args = [spread_maps, upd]
    if before is not None:
        in_specs.append(block)
        args.append(before)
    return pl.pallas_call(
        functools.partial(scatter_kernel, block_rows, tile, odd, chunk),
        grid_spec=pltpu.PrefetchScalarGridSpec(
            num_scalar_prefetch=2,
            grid=(count, block_rows // tile),
            in_specs=in_specs,
            out_specs=block,
        ),
        out_shape=jax.ShapeDtypeStruct((count, m, block_rows), BF16),
        compiler_params=params(),
        cost_estimate=cost(2 * m * u * count * block_rows, 4 * m * count * block_rows),
    )(row, order, *args)


def gather_kernel(block_rows, tile, which, chunk, *refs):
    row_ref, order_ref, map_ref, *rest = refs
    blocks, o_ref = rest[: len(which)], rest[-1]
    slot_map = map_ref[0]
    total = None
    for block_ref, j in zip(blocks, which):
        first = lax.bitwise_xor(row_ref[0], j) * block_rows
        for start in range(0, block_rows, tile):
            local = (slot_map - (first + start)).astype(I16)
            row_ids = lax.broadcasted_iota(I16, (tile, slot_map.shape[1]), 0)
            hot = jnp.where(row_ids == local, BF16(1), BF16(0))
            term = lax.dot_general(
                block_ref[:, start : start + tile], hot, NN, preferred_element_type=F32
            )
            total = term if total is None else total + term
    before = rest[len(which)] if len(rest) == len(which) + 2 else None

    def store(ds, value):
        if before is not None:
            value = value + before[ds, :].astype(F32)
        o_ref[ds, :] = value.astype(o_ref.dtype)

    store_in_order(order_ref, chunk, store, total)


def gather(blocks, which, maps, child, row, order, before):
    m, block_rows = blocks[0].shape
    u = maps.shape[2]
    tile = tile_of(block_rows, 512, 384, 256, 128)
    bu = tile_of(u, 512, 384, 256, 128)
    chunk = m // order.shape[0]
    in_specs = [pl.BlockSpec((1, 1, bu), lambda i, r, o: (child, 0, i))]
    in_specs += [pl.BlockSpec((m, block_rows), lambda i, r, o: (0, 0))] * len(blocks)
    out_block = pl.BlockSpec((m, bu), lambda i, r, o: (0, i))
    args = [maps, *blocks]
    if before is not None:
        in_specs.append(out_block)
        args.append(before)
    return pl.pallas_call(
        functools.partial(gather_kernel, block_rows, tile, which, chunk),
        grid_spec=pltpu.PrefetchScalarGridSpec(
            num_scalar_prefetch=2, grid=(u // bu,), in_specs=in_specs, out_specs=out_block
        ),
        out_shape=jax.ShapeDtypeStruct((m, u), BF16),
        compiler_params=params(),
        cost_estimate=cost(
            2 * m * u * len(blocks) * block_rows, 2 * m * len(blocks) * block_rows
        ),
    )(row, order, *args)


def reorder_kernel(order_ref, x_ref, o_ref):
    o_ref[...] = x_ref[...].astype(o_ref.dtype)


def reorder(x, order):
    m, n = x.shape
    chunk = m // order.shape[0]
    return pl.pallas_call(
        reorder_kernel,
        grid_spec=pltpu.PrefetchScalarGridSpec(
            num_scalar_prefetch=1,
            grid=(order.shape[0],),
            in_specs=[pl.BlockSpec((chunk, n), lambda i, o: (i, 0))],
            out_specs=pl.BlockSpec((chunk, n), lambda i, o: (o[i], 0)),
        ),
        out_shape=jax.ShapeDtypeStruct((m, n), F32),
        compiler_params=params(),
        cost_estimate=cost(m * n, 6 * m * n),
    )(order, x)


def join_kernel(sign, *refs):
    x_ref, y_ref, *rest = refs
    wide_ref, narrow_ref = rest[-2:]
    total = x_ref[...].astype(F32) + sign * y_ref[...].astype(F32)
    wide_ref[...] = total
    narrow_ref[...] = total.astype(BF16)


def join(x, y, after=()):
    whole = pl.BlockSpec(x.shape, lambda: (0, 0))
    return pl.pallas_call(
        functools.partial(join_kernel, 1),
        in_specs=[whole, whole] + [ANY] * len(after),
        out_specs=[whole, whole],
        out_shape=[jax.ShapeDtypeStruct(x.shape, F32), jax.ShapeDtypeStruct(x.shape, BF16)],
        compiler_params=params(),
        cost_estimate=cost(x.size, 12 * x.size),
    )(x, y, *after)


def swap(x, axis, bit, size):
    return lax.ppermute(x, axis, [(i, i ^ bit) for i in range(size)])


def add(x, y):
    return x.astype(F32) + y.astype(F32)


def bits(size):
    return [1 << b for b in range(size.bit_length() - 1)]


def on_device(sizes, child_loads, child_inverse, child_panel, child_map, root_loads, root_inverse):
    leafs, rows, cols = sizes
    kids = child_loads.shape[0]
    case_count, root_rows = root_loads.shape
    leaf, row, col = (lax.axis_index(a).astype(jnp.int32) for a in ("leaf", "row", "col"))
    core = lax.bitwise_and(row, 1)[None]
    row_1 = row[None]
    root_w = root_inverse[None]
    piece = case_count // (leafs * cols)
    wide = rows == 4 and cols == 2 and piece % 16 == 0 and root_rows % 256 == 0

    def to_row(x, bit):
        return swap(x, "row", bit, rows)

    def to_col(x, bit=1):
        return swap(x, "col", bit, cols)

    def to_leaf(x, j):
        return swap(x, "leaf", j, leafs)

    def row_sum(x, w, child, split, after=()):
        if split:
            (sent,) = nn(x, w, child, core, (1,), after)
            (kept,) = nn(x, w, child, core, (0,), (sent,))
        else:
            sent, kept = nn(x, w, child, core, (1, 0), after)
        return join(kept, to_row(sent, 1))

    def row_end(total, narrow, after=()):
        for bit in bits(rows)[1:]:
            total, narrow = join(total, to_row(narrow, bit), after)
        return total, narrow

    def halves(rounded):
        return rounded, to_row(rounded, 1)

    slot_rows = child_panel.shape[1]
    own_map = lax.dynamic_slice_in_dim(child_map, row * slot_rows, slot_rows, 1)
    maps = own_map.reshape(kids, 1, slot_rows)
    spread_maps = spread(maps)

    if wide:
        ids = jnp.arange(cols * leafs, dtype=jnp.int32)
        order = lax.bitwise_xor(ids, col * leafs + leaf)
    else:
        order = jnp.zeros((1,), jnp.int32)

    begun = []
    after = ()
    for k in range(kids):
        begun.append(row_sum(child_loads, child_inverse, k, k == 0, after))
        after = begun[k][1:]
    forward = []
    sent = kept = None
    for k in range(kids):
        total, rounded = row_end(*begun[k], after if k == 0 else (sent, kept))
        forward.append(total)
        upd = nt(*halves(rounded), child_panel, k, core)
        sent = scatter(upd, spread_maps, k, row_1, order, rows, root_rows, 1, sent)
        kept = scatter(upd, spread_maps, k, row_1, order, rows, root_rows, 0, kept)

    total = add(kept, to_row(sent, 1))
    if wide:
        half, cut = case_count // 2, root_rows // 2
        left = add(total[:, :half, :cut], to_col(total[:, half:, :cut].astype(BF16)))
        right = add(total[0, :, cut:], to_row(total[1, :, cut:].astype(BF16), 2))
        left = add(left[0], to_row(left[1].astype(BF16), 2))
        right = add(right[:half], to_col(right[half:].astype(BF16)))
        total = jnp.concatenate([left, right], axis=1)
        narrow = total.astype(BF16)
        mine_cases = total[:piece]
        for j in range(1, leafs):
            away = narrow[j * piece : (j + 1) * piece]
            mine_cases = add(mine_cases, to_leaf(away, j))
        first_case = (col * leafs + leaf) * piece
        loads = lax.dynamic_slice_in_dim(root_loads, first_case, piece, 0)
        residual = (loads.astype(F32) - mine_cases).astype(BF16)
        residual = jnp.concatenate([residual, to_col(residual)])
    else:
        for bit in bits(rows)[1:]:
            total = add(total[0::2], to_row(total[1::2].astype(BF16), bit))
        total = total[0]
        chunk = case_count // leafs

        def cases_of(x, j):
            return lax.dynamic_slice_in_dim(x, lax.bitwise_xor(leaf, j) * chunk, chunk, 0)

        narrow = total.astype(BF16)
        mine_cases = cases_of(total, 0)
        for j in range(1, leafs):
            mine_cases = add(mine_cases, to_leaf(cases_of(narrow, j), j))
        for bit in bits(cols):
            narrow = mine_cases.astype(BF16)
            mine_cases = add(narrow, to_col(narrow, bit))
        residual = (cases_of(root_loads, 0).astype(F32) - mine_cases).astype(BF16)

    _, root_forward = row_end(*row_sum(residual, root_w, 0, False))
    part = nt(*halves(root_forward), root_w, 0, core)

    picked = [None] * kids
    if wide:
        part = add(part[:piece], to_col(part[piece:])).astype(BF16)
        held = jnp.concatenate([part] + [to_leaf(part, j) for j in range(1, leafs)])
        beside, across = to_col(held), to_row(held, 2)
        near = jnp.concatenate([held, beside])
        near_other = to_row(near, 1)
        cut = held.shape[0] // 2
        far = jnp.concatenate([across, to_col(across[:cut]), to_row(beside[cut:], 2)])
        far_other = to_row(far, 1)
        root_solution = reorder(near, order)
        for k in range(kids):
            picked[k] = gather([near, near_other], [0, 1], maps, k, row_1, order, None)
        last_blocks, last_at = [far, far_other], [2, 3]
    else:
        for bit in bits(cols):
            part = add(part, to_col(part, bit)).astype(BF16)
        own = jnp.zeros((case_count, root_rows), BF16)
        for j in range(leafs):
            got = part if j == 0 else to_leaf(part, j)
            own = lax.dynamic_update_slice_in_dim(
                own, got, lax.bitwise_xor(leaf, j) * (case_count // leafs), 0
            )
        root_solution = own.astype(F32)
        groups = [own]
        for bit in [1, *bits(rows)[1:]]:
            got = to_row(jnp.stack(groups), bit)
            groups += [got[i] for i in range(len(groups))]
        last_blocks, last_at = groups, list(range(rows))

    begun = []
    after = ()
    for k in range(kids):
        full = gather(last_blocks, last_at, maps, k, row_1, order, picked[k])
        begun.append(row_sum(full, child_panel, k, k == 0, after))
        after = begun[k][1:]
    solved = []
    for k in range(kids):
        back, _ = row_end(*begun[k], after)
        pair = halves((forward[k] - back).astype(BF16))
        chunks = 2 if k == kids - 1 and slot_rows % 256 == 0 else 1
        outs = []
        for at in range(chunks):
            out = nt(*pair, child_inverse, k, core, at, chunks)
            after = (out,)
            for bit in bits(cols):
                out = add(out.astype(BF16), to_col(out.astype(BF16), bit))
            outs.append(out)
        solved.append(jnp.concatenate(outs, axis=1) if chunks > 1 else outs[0])
    return (jnp.stack(solved), root_solution)


def solution(mesh):
    sizes = tuple(mesh.shape[a] for a in ("leaf", "row", "col"))
    in_specs = (
        P("leaf", None, "row"),
        P("leaf", "row", "col"),
        P("leaf", "row", "col"),
        P("leaf", None),
        P(None, "row"),
        P("row", "col"),
    )
    out_specs = (P("leaf", None, "row"), P(None, "row"))
    return jax.shard_map(
        functools.partial(on_device, sizes),
        mesh=mesh,
        in_specs=in_specs,
        out_specs=out_specs,
        check_vma=False,
    )
```

```python
import functools

import jax
import jax.numpy as jnp
from jax import lax
from jax.experimental import pallas as pl
from jax.experimental.pallas import tpu as pltpu
from jax.sharding import PartitionSpec as P

BF16 = jnp.bfloat16
F32 = jnp.float32
I16 = jnp.int16
NN = (((1,), (0,)), ((), ()))
NT = (((1,), (1,)), ((), ()))
LANES = 128
ANY = pl.BlockSpec(memory_space=pl.ANY)
WHOLE = pl.BlockSpec(memory_space=pltpu.VMEM)
SCALARS = pl.BlockSpec(memory_space=pltpu.SMEM)


def tile_of(extent, *sizes):
    for size in sizes:
        if extent % size == 0:
            return size
    return extent


def params():
    return pltpu.CompilerParams(vmem_limit_bytes=10 * 1024 * 1024)


def cost(flops, nbytes):
    return pl.CostEstimate(flops=flops // 64, bytes_accessed=nbytes // 64, transcendentals=0)


def in_hbm(w):
    return pltpu.with_memory_space_constraint(w, pltpu.HBM)


def in_vmem(w):
    return pltpu.with_memory_space_constraint(w, pltpu.VMEM)


def preload_kernel(child, w_ref, *rest):
    o_ref, sem = rest[-2:]
    copy = pltpu.make_async_copy(w_ref.at[child], o_ref, sem)
    copy.start()
    copy.wait()


def preload(w, child, after=()):
    return pl.pallas_call(
        functools.partial(preload_kernel, child),
        in_specs=[pl.BlockSpec(memory_space=pltpu.HBM)] + [ANY] * len(after),
        out_specs=WHOLE,
        out_shape=pltpu.VMEM(w.shape[1:], w.dtype),
        scratch_shapes=[pltpu.SemaphoreType.DMA],
        compiler_params=params(),
        cost_estimate=cost(0, w[0].size * 2),
    )(in_hbm(w), *after)


def put_pieces(refs, value):
    rows = value.shape[0] // len(refs)
    for i, ref in enumerate(refs):
        ref[...] = value[i * rows : (i + 1) * rows].astype(ref.dtype)


def take_pieces(refs):
    return refs[0][...] if len(refs) == 1 else jnp.concatenate([r[...] for r in refs], axis=0)


def nn_kernel(half_ref, x_ref, w_ref, *outs):
    x = x_ref[0] if len(x_ref.shape) == 3 else x_ref[...]
    product = lax.dot_general(x, w_ref[0], NN, preferred_element_type=F32)
    put_pieces(outs, product)


def nn(x, w, child, core, part, pieces=1, after=()):
    m, k = x.shape[-2:]
    n_half = w.shape[2] // 2
    bn = tile_of(n_half, 768, 512, 384, 256, 128)
    steps = n_half // bn
    if x.ndim == 3:
        x_spec = pl.BlockSpec((1, m, k), lambda i, h: (child, 0, 0))
        x = in_hbm(x)
    else:
        x_spec = pl.BlockSpec((m, k), lambda i, h: (0, 0))

    def kernel(half_ref, x_ref, w_ref, *rest):
        nn_kernel(half_ref, x_ref, w_ref, *rest[len(after) :])

    return pl.pallas_call(
        kernel,
        grid_spec=pltpu.PrefetchScalarGridSpec(
            num_scalar_prefetch=1,
            grid=(steps,),
            in_specs=[
                x_spec,
                pl.BlockSpec(
                    (1, k, bn), lambda i, h: (child, 0, lax.bitwise_xor(h[0], part) * steps + i)
                ),
            ]
            + [ANY] * len(after),
            out_specs=[pl.BlockSpec((m // pieces, bn), lambda i, h: (0, i))] * pieces,
        ),
        out_shape=[jax.ShapeDtypeStruct((m // pieces, n_half), BF16 if part else F32)] * pieces,
        compiler_params=params(),
        cost_estimate=cost(2 * m * k * n_half, 2 * k * n_half),
    )(core, x, in_hbm(w), *after)


def held_nn(x, w, core, part, pieces=1, after=()):
    m, k = x.shape
    n_half = w.shape[1] // 2
    bn = tile_of(n_half, 512, 384, 256, 128)

    def kernel(half_ref, x_ref, w_ref, *rest):
        outs = rest[len(after) :]
        base = lax.bitwise_xor(half_ref[0], part) * n_half
        x = x_ref[...]
        for start in range(0, n_half, bn):
            cols = pl.ds(pl.multiple_of(base + start, LANES), bn)
            product = lax.dot_general(x, w_ref[:, cols], NN, preferred_element_type=F32)
            for i, out in enumerate(outs):
                rows = m // pieces
                out[:, start : start + bn] = product[i * rows : (i + 1) * rows].astype(out.dtype)

    return pl.pallas_call(
        kernel,
        in_specs=[SCALARS, WHOLE, WHOLE] + [ANY] * len(after),
        out_specs=[WHOLE] * pieces,
        out_shape=[jax.ShapeDtypeStruct((m // pieces, n_half), BF16 if part else F32)] * pieces,
        compiler_params=params(),
        cost_estimate=cost(2 * m * k * n_half, 2 * k * n_half),
    )(core, x, in_vmem(w), *after)


def held_nt(mine, other, w, core, chunk=0, chunks=1, after=()):
    m = sum(x.shape[0] for x in mine)
    k_half = mine[0].shape[1]
    u = w.shape[0] // chunks
    bu = tile_of(u, 512, 384, 256, 128)
    first = chunk * u

    def kernel(half_ref, *refs):
        a = take_pieces(refs[: len(mine)])
        b = take_pieces(refs[len(mine) : len(mine) + len(other)])
        w_ref, o_ref = refs[len(mine) + len(other)], refs[-1]
        low = half_ref[0] == 0
        left, right = jnp.where(low, a, b), jnp.where(low, b, a)
        for start in range(0, u, bu):
            at = slice(first + start, first + start + bu)
            total = lax.dot_general(left, w_ref[at, :k_half], NT, preferred_element_type=F32)
            total += lax.dot_general(right, w_ref[at, k_half:], NT, preferred_element_type=F32)
            o_ref[:, start : start + bu] = total.astype(o_ref.dtype)

    return pl.pallas_call(
        kernel,
        in_specs=[SCALARS] + [WHOLE] * (len(mine) + len(other) + 1) + [ANY] * len(after),
        out_specs=WHOLE,
        out_shape=jax.ShapeDtypeStruct((m, u), BF16),
        compiler_params=params(),
        cost_estimate=cost(4 * m * k_half * u, 4 * k_half * u),
    )(core, *mine, *other, in_vmem(w), *after)


def spread_kernel(map_ref, o_ref):
    u = map_ref.shape[2]
    step = tile_of(u, LANES)
    for start in range(0, u, step):
        row = map_ref[0, :, start : start + step]
        o_ref[0, start : start + step, :] = jnp.broadcast_to(row, (LANES, step)).T.astype(I16)


def spread(maps):
    kids, _, u = maps.shape
    return pl.pallas_call(
        spread_kernel,
        grid=(kids,),
        in_specs=[pl.BlockSpec((1, 1, u), lambda k: (k, 0, 0))],
        out_specs=pl.BlockSpec((1, u, LANES), lambda k: (k, 0, 0)),
        out_shape=jax.ShapeDtypeStruct((kids, u, LANES), I16),
        compiler_params=params(),
        cost_estimate=cost(kids * u * LANES, 2 * kids * u * LANES),
    )(maps)


def store_in_order(order_ref, chunk, store, value):
    for i in range(value.shape[0] // chunk):
        store(
            pl.ds(pl.multiple_of(order_ref[i] * chunk, chunk), chunk),
            value[i * chunk : (i + 1) * chunk],
        )


def scatter_kernel(block_rows, tile, odd, chunk, *refs):
    row_ref, order_ref, map_ref, upd_ref, *rest = refs
    o_ref = rest[-1]
    j, t = pl.program_id(0), pl.program_id(1)
    dest = lax.bitwise_xor(row_ref[0], 2 * j + odd)
    first = (dest * block_rows + t * tile).astype(I16)
    local = map_ref[0] - first
    u = local.shape[0]
    sub = tile_of(tile, 256, 128)
    upd = upd_ref[...]
    for start in range(0, tile, sub):
        wide = jnp.concatenate([local] * (sub // LANES), axis=1)
        row_ids = lax.broadcasted_iota(I16, (u, sub), 1) + jnp.int16(start)
        hot = jnp.where(row_ids == wide, BF16(1), BF16(0))
        total = lax.dot_general(upd, hot, NN, preferred_element_type=F32)
        if len(rest) == 2:
            at = slice(start, start + sub)
            before = rest[0]

            def store(ds, value, at=at, before=before):
                o_ref[0, ds, at] = (value + before[0, ds, at].astype(F32)).astype(o_ref.dtype)

        else:
            at = slice(start, start + sub)

            def store(ds, value, at=at):
                o_ref[0, ds, at] = value.astype(o_ref.dtype)

        store_in_order(order_ref, chunk, store, total)


def scatter(upd, spread_maps, child, row, order, rows_count, block_rows, odd, before):
    m, u = upd.shape
    tile = tile_of(block_rows, 768, 512, 384, 256, 128)
    count = rows_count // 2
    chunk = m // order.shape[0]
    block = pl.BlockSpec((1, m, tile), lambda j, t, r, o: (j, 0, t))
    in_specs = [
        pl.BlockSpec((1, u, LANES), lambda j, t, r, o: (child, 0, 0)),
        pl.BlockSpec((m, u), lambda j, t, r, o: (0, 0)),
    ]
    args = [spread_maps, upd]
    if before is not None:
        in_specs.append(block)
        args.append(before)
    return pl.pallas_call(
        functools.partial(scatter_kernel, block_rows, tile, odd, chunk),
        grid_spec=pltpu.PrefetchScalarGridSpec(
            num_scalar_prefetch=2,
            grid=(count, block_rows // tile),
            in_specs=in_specs,
            out_specs=block,
        ),
        out_shape=jax.ShapeDtypeStruct((count, m, block_rows), BF16),
        compiler_params=params(),
        cost_estimate=cost(2 * m * u * count * block_rows, 4 * m * count * block_rows),
    )(row, order, *args)


def gather_kernel(block_rows, tile, which, counts, chunk, added, row_ref, order_ref, map_ref, *rest):
    o_ref = rest[-1]
    slot_map = map_ref[0]
    total, at = None, 0
    for j, count in zip(which, counts):
        pieces = rest[at : at + count]
        at += count
        first = lax.bitwise_xor(row_ref[0], j) * block_rows
        for start in range(0, block_rows, tile):
            local = (slot_map - (first + start)).astype(I16)
            row_ids = lax.broadcasted_iota(I16, (tile, slot_map.shape[1]), 0)
            hot = jnp.where(row_ids == local, BF16(1), BF16(0))
            block = [p[:, start : start + tile] for p in pieces]
            block = block[0] if count == 1 else jnp.concatenate(block, axis=0)
            term = lax.dot_general(block, hot, NN, preferred_element_type=F32)
            total = term if total is None else total + term

    def store(ds, value):
        if added:
            value = value + rest[at][ds, :].astype(F32)
        o_ref[ds, :] = value.astype(o_ref.dtype)

    store_in_order(order_ref, chunk, store, total)


def gather(blocks, which, maps, child, row, order, before, after=()):
    m = sum(p.shape[0] for p in blocks[0])
    block_rows = blocks[0][0].shape[1]
    u = maps.shape[2]
    tile = tile_of(block_rows, 512, 384, 256, 128)
    bu = tile_of(u, 512, 384, 256, 128)
    chunk = m // order.shape[0]
    counts = [len(b) for b in blocks]
    in_specs = [pl.BlockSpec((1, 1, bu), lambda i, r, o: (child, 0, i))]
    args = [maps]
    for p in (p for b in blocks for p in b):
        in_specs.append(pl.BlockSpec(p.shape, lambda i, r, o: (0, 0)))
        args.append(p)
    out_block = pl.BlockSpec((m, bu), lambda i, r, o: (0, i))
    if before is not None:
        in_specs.append(out_block)
        args.append(before)
    in_specs += [ANY] * len(after)
    return pl.pallas_call(
        functools.partial(
            gather_kernel, block_rows, tile, which, counts, chunk, before is not None
        ),
        grid_spec=pltpu.PrefetchScalarGridSpec(
            num_scalar_prefetch=2, grid=(u // bu,), in_specs=in_specs, out_specs=out_block
        ),
        out_shape=jax.ShapeDtypeStruct((m, u), BF16),
        compiler_params=params(),
        cost_estimate=cost(
            2 * m * u * len(blocks) * block_rows, 2 * m * len(blocks) * block_rows
        ),
    )(row, order, *args, *after)


def finish(held, kids, child, chunk, chunks, terms):
    m, n = terms[0].shape
    place = pl.BlockSpec((1, m, n), lambda i: (child, 0, chunk))
    whole = pl.BlockSpec((m, n), lambda i: (0, 0))

    def kernel(*refs):
        total = refs[0][...].astype(F32)
        for ref in refs[1 : len(terms)]:
            total += ref[...].astype(F32)
        refs[-1][0] = total

    extra = () if held is None else (held,)
    return pl.pallas_call(
        kernel,
        grid=(1,),
        in_specs=[whole] * len(terms) + [ANY] * len(extra),
        out_specs=place,
        out_shape=jax.ShapeDtypeStruct((kids, m, n * chunks), F32),
        input_output_aliases={len(terms): 0} if extra else {},
        compiler_params=params(),
        cost_estimate=cost(m * n, 8 * m * n),
    )(*terms, *extra)


def reorder(pieces, order):
    m, n = sum(p.shape[0] for p in pieces), pieces[0].shape[1]
    chunk = m // order.shape[0]

    def kernel(order_ref, *refs):
        def store(ds, value):
            refs[-1][ds, :] = value

        store_in_order(order_ref, chunk, store, take_pieces(refs[:-1]).astype(F32))

    return pl.pallas_call(
        kernel,
        in_specs=[SCALARS] + [WHOLE] * len(pieces),
        out_specs=WHOLE,
        out_shape=jax.ShapeDtypeStruct((m, n), F32),
        compiler_params=params(),
        cost_estimate=cost(m * n, 6 * m * n),
    )(order, *pieces)


def join(terms, signs, after=(), wide=True, narrow=1):
    m = sum(x.shape[0] for x in terms[0])
    n = terms[0][0].shape[1]
    counts = [len(t) for t in terms]

    def kernel(*refs):
        outs = refs[sum(counts) + len(after) :]
        total, at = None, 0
        for count, sign in zip(counts, signs):
            value = take_pieces(refs[at : at + count]).astype(F32)
            at += count
            value = value if sign > 0 else -value
            total = value if total is None else total + value
        if wide:
            outs[0][...] = total
            outs = outs[1:]
        if narrow:
            put_pieces(outs, total)

    shapes = [jax.ShapeDtypeStruct((m, n), F32)] if wide else []
    shapes += [jax.ShapeDtypeStruct((m // narrow, n), BF16)] * narrow if narrow else []
    outs = pl.pallas_call(
        kernel,
        in_specs=[WHOLE] * sum(counts) + [ANY] * len(after),
        out_specs=[WHOLE] * len(shapes),
        out_shape=shapes,
        compiler_params=params(),
        cost_estimate=cost(m * n, 12 * m * n),
    )(*[x for t in terms for x in t], *after)
    return (outs[0] if wide else None), (outs[1:] if wide else outs)


def swap(x, axis, bit, size):
    return lax.ppermute(x, axis, [(i, i ^ bit) for i in range(size)])


def add(x, y):
    return x.astype(F32) + y.astype(F32)


def bits(size):
    return [1 << b for b in range(size.bit_length() - 1)]


def on_device(sizes, child_loads, child_inverse, child_panel, child_map, root_loads, root_inverse):
    leafs, rows, cols = sizes
    kids = child_loads.shape[0]
    case_count, root_rows = root_loads.shape
    leaf, row, col = (lax.axis_index(a).astype(jnp.int32) for a in ("leaf", "row", "col"))
    core = lax.bitwise_and(row, 1)[None]
    row_1 = row[None]
    root_w = root_inverse[None]
    piece = case_count // (leafs * cols)
    wide = rows == 4 and cols == 2 and piece % 16 == 0 and root_rows % 256 == 0

    def to_row(x, bit):
        return swap(x, "row", bit, rows)

    def to_col(x, bit=1):
        return swap(x, "col", bit, cols)

    def to_leaf(x, j):
        return swap(x, "leaf", j, leafs)

    def pieces_of(k, m=case_count):
        return 4 if k and m % 64 == 0 else 1

    def core_sum(kept, sent):
        total, narrow = join([[kept], [to_row(x, 1) for x in sent]], (1, 1))
        return total, narrow[0]

    def row_end(total, narrow, after=(), base=None, wide=True, pieces=1):
        steps = bits(rows)[1:]
        for at, bit in enumerate(steps):
            last = at == len(steps) - 1
            terms, signs = [[total], [to_row(narrow, bit)]], (1, 1)
            if last and base is not None:
                terms, signs = [[base], *terms], (1, -1, -1)
            total, out = join(
                terms, signs, after, wide or not last, pieces if last else 1
            )
            narrow = out[0]
        return total, out

    def halves(rounded):
        return rounded, [to_row(x, 1) for x in rounded]

    slot_rows = child_panel.shape[1]
    own_map = lax.dynamic_slice_in_dim(child_map, row * slot_rows, slot_rows, 1)
    maps = own_map.reshape(kids, 1, slot_rows)
    spread_maps = spread(maps)

    if wide:
        ids = jnp.arange(cols * leafs, dtype=jnp.int32)
        order = lax.bitwise_xor(ids, col * leafs + leaf)
    else:
        order = jnp.zeros((1,), jnp.int32)

    begun = []
    after = ()
    for k in range(kids):
        sent = nn(child_loads, child_inverse, k, core, 1, pieces_of(k))
        kept = nn(child_loads, child_inverse, k, core, 0, 1, (sent[0], *after))
        begun.append(core_sum(kept[0], sent))
        after = begun[k][1:]
    panels = []
    for k in range(kids):
        panels.append(preload(child_panel, k, after))
        after = (panels[k],)
    forward = []
    sent = kept = None
    for k in range(kids):
        after = after if k == 0 else (sent,)
        total, rounded = row_end(*begun[k], after, pieces=pieces_of(k == 0))
        forward.append(total)
        upd = held_nt(*halves(rounded), panels[k], core)
        sent = scatter(upd, spread_maps, k, row_1, order, rows, root_rows, 1, sent)
        kept = scatter(upd, spread_maps, k, row_1, order, rows, root_rows, 0, kept)

    total = add(kept, to_row(sent, 1))
    if wide:
        half, cut = case_count // 2, root_rows // 2
        left = add(total[:, :half, :cut], to_col(total[:, half:, :cut].astype(BF16)))
        right = add(total[0, :, cut:], to_row(total[1, :, cut:].astype(BF16), 2))
        left = add(left[0], to_row(left[1].astype(BF16), 2))
        right = add(right[:half], to_col(right[half:].astype(BF16)))
        total = jnp.concatenate([left, right], axis=1)
        narrow = total.astype(BF16)
        shares = [narrow[j * piece : (j + 1) * piece] for j in range(1, leafs)]
        root_held = preload(root_w, 0, shares)
        first_case = (col * leafs + leaf) * piece
        loads = lax.dynamic_slice_in_dim(root_loads, first_case, piece, 0)
        terms = [loads, total[:piece]] + [to_leaf(x, j + 1) for j, x in enumerate(shares)]
        _, (residual,) = join([[x] for x in terms], (1,) + (-1,) * leafs, (root_held,), False)
        residual = jnp.concatenate([residual, to_col(residual)])
    else:
        for bit in bits(rows)[1:]:
            total = add(total[0::2], to_row(total[1::2].astype(BF16), bit))
        total = total[0]
        chunk = case_count // leafs

        def cases_of(x, j):
            return lax.dynamic_slice_in_dim(x, lax.bitwise_xor(leaf, j) * chunk, chunk, 0)

        narrow = total.astype(BF16)
        mine_cases = cases_of(total, 0)
        for j in range(1, leafs):
            mine_cases = add(mine_cases, to_leaf(cases_of(narrow, j), j))
        for bit in bits(cols):
            narrow = mine_cases.astype(BF16)
            mine_cases = add(narrow, to_col(narrow, bit))
        residual = (cases_of(root_loads, 0).astype(F32) - mine_cases).astype(BF16)

    if not wide:
        root_held = preload(root_w, 0, (kept,))
    sent = held_nn(residual, root_held, core, 1)
    kept = held_nn(residual, root_held, core, 0, 1, sent)
    begun = core_sum(kept[0], sent)
    panels = [preload(child_panel, 0, begun[1:])]
    _, root_forward = row_end(*begun, (panels[0],), wide=False)
    part = held_nt(*halves(root_forward), root_held, core)
    panels += [preload(child_panel, k, (part,)) for k in range(1, kids)]

    picked = [None] * kids
    if wide:
        _, (part,) = join(
            [[part[:piece]], [to_col(part[piece:])]], (1, 1), tuple(panels[1:]), False
        )
        inverses = [preload(child_inverse, 0, (part,))]
        shares = [part] + [to_leaf(part, j) for j in range(1, leafs)]
        _, (held,) = join([shares], (1,), tuple(inverses), False)
        inverses += [preload(child_inverse, k, (held,)) for k in range(1, kids)]
        beside, across = to_col(held), to_row(held, 2)
        cut = held.shape[0] // 2
        _, near = join([[held, beside]], (1,), tuple(inverses[1:]), False, 4)
        near_other = [to_row(x, 1) for x in near]
        rest = [to_col(across[:cut]), to_row(beside[cut:], 2)]
        for k in range(kids):
            picked[k] = gather([near, near_other], [0, 1], maps, k, row_1, order, None, (across,))
        _, far = join([[across, *rest]], (1,), tuple(picked), False)
        far_other = [to_row(x, 1) for x in far]
        root_solution = reorder(near, order)
        last_blocks, last_at = [far, far_other], [2, 3]
    else:
        inverses = [preload(child_inverse, k, (part,)) for k in range(kids)]
        for bit in bits(cols):
            part = add(part, to_col(part, bit)).astype(BF16)
        own = jnp.zeros((case_count, root_rows), BF16)
        for j in range(leafs):
            got = part if j == 0 else to_leaf(part, j)
            own = lax.dynamic_update_slice_in_dim(
                own, got, lax.bitwise_xor(leaf, j) * (case_count // leafs), 0
            )
        root_solution = own.astype(F32)
        groups = [own]
        for bit in [1, *bits(rows)[1:]]:
            got = to_row(jnp.stack(groups), bit)
            groups += [got[i] for i in range(len(groups))]
        last_blocks, last_at = [[g] for g in groups], list(range(rows))

    begun = []
    after = ()
    for k in range(kids):
        full = gather(last_blocks, last_at, maps, k, row_1, order, picked[k], after)
        sent = held_nn(full, panels[k], core, 1, pieces_of(k))
        kept = held_nn(full, panels[k], core, 0, 1, sent[:1])
        begun.append(core_sum(kept[0], sent))
        after = begun[k][1:]
    solved = None
    chunks = 2 if slot_rows % 256 == 0 else 1
    after = (root_solution, *after)
    for k in range(kids):
        _, rounded = row_end(*begun[k], after, forward[k], False, pieces_of(k == 0))
        pair = halves(rounded)
        for at in range(chunks):
            out = held_nt(*pair, inverses[k], core, at, chunks)
            after = (out,)
            terms = [out, to_col(out)]
            for bit in bits(cols)[1:]:
                out = add(*terms).astype(BF16)
                terms = [out, to_col(out, bit)]
            solved = finish(solved, kids, k, at, chunks, terms)
    return (solved, root_solution)


def solution(mesh):
    sizes = tuple(mesh.shape[a] for a in ("leaf", "row", "col"))
    in_specs = (
        P("leaf", None, "row"),
        P("leaf", "row", "col"),
        P("leaf", "row", "col"),
        P("leaf", None),
        P(None, "row"),
        P("row", "col"),
    )
    out_specs = (P("leaf", None, "row"), P(None, "row"))
    return jax.shard_map(
        functools.partial(on_device, sizes),
        mesh=mesh,
        in_specs=in_specs,
        out_specs=out_specs,
        check_vma=False,
    )
```

```python
import functools

import jax
import jax.numpy as jnp
from jax import lax
from jax.experimental import pallas as pl
from jax.experimental.pallas import tpu as pltpu
from jax.sharding import PartitionSpec as P

BF16 = jnp.bfloat16
F32 = jnp.float32
I16 = jnp.int16
NN = (((1,), (0,)), ((), ()))
NT = (((1,), (1,)), ((), ()))
LANES = 128
ANY = pl.BlockSpec(memory_space=pl.ANY)
WHOLE = pl.BlockSpec(memory_space=pltpu.VMEM)
SCALARS = pl.BlockSpec(memory_space=pltpu.SMEM)
IN_HBM = pl.BlockSpec(memory_space=pltpu.HBM)


def tile_of(extent, *sizes):
    for size in sizes:
        if extent % size == 0:
            return size
    return extent


def params():
    return pltpu.CompilerParams(vmem_limit_bytes=10 * 1024 * 1024)


def cost(flops, nbytes):
    return pl.CostEstimate(flops=flops // 64, bytes_accessed=nbytes // 64, transcendentals=0)


def in_hbm(w):
    return pltpu.with_memory_space_constraint(w, pltpu.HBM)


def in_vmem(w):
    return pltpu.with_memory_space_constraint(w, pltpu.VMEM)


TOKEN = jax.ShapeDtypeStruct((8, LANES), F32)


def preload_kernel(child, w_ref, *rest):
    o_ref, token_ref, sem = rest[-3:]
    copy = pltpu.make_async_copy(w_ref.at[child], o_ref, sem)
    copy.start()
    token_ref[...] = jnp.zeros_like(token_ref)
    copy.wait()


def preload(w, child, after=()):
    return pl.pallas_call(
        functools.partial(preload_kernel, child),
        in_specs=[pl.BlockSpec(memory_space=pltpu.HBM)] + [ANY] * len(after),
        out_specs=[WHOLE, WHOLE],
        out_shape=[pltpu.VMEM(w.shape[1:], w.dtype), TOKEN],
        scratch_shapes=[pltpu.SemaphoreType.DMA],
        compiler_params=params(),
        cost_estimate=cost(0, w[0].size * 2),
    )(in_hbm(w), *after)


def put_pieces(refs, value):
    rows = value.shape[0] // len(refs)
    for i, ref in enumerate(refs):
        ref[...] = value[i * rows : (i + 1) * rows].astype(ref.dtype)


def take_pieces(refs):
    return refs[0][...] if len(refs) == 1 else jnp.concatenate([r[...] for r in refs], axis=0)


def nn_kernel(half_ref, x_ref, w_ref, *outs):
    x = x_ref[0] if len(x_ref.shape) == 3 else x_ref[...]
    product = lax.dot_general(x, w_ref[0], NN, preferred_element_type=F32)
    put_pieces(outs, product)


def nn(x, w, child, core, part, pieces=1, after=()):
    m, k = x.shape[-2:]
    n_half = w.shape[2] // 2
    bn = tile_of(n_half, 768, 512, 384, 256, 128)
    steps = n_half // bn
    if x.ndim == 3:
        x_spec = pl.BlockSpec((1, m, k), lambda i, h: (child, 0, 0))
        x = in_hbm(x)
    else:
        x_spec = pl.BlockSpec((m, k), lambda i, h: (0, 0))

    def kernel(half_ref, x_ref, w_ref, *rest):
        nn_kernel(half_ref, x_ref, w_ref, *rest[len(after) :])

    return pl.pallas_call(
        kernel,
        grid_spec=pltpu.PrefetchScalarGridSpec(
            num_scalar_prefetch=1,
            grid=(steps,),
            in_specs=[
                x_spec,
                pl.BlockSpec(
                    (1, k, bn), lambda i, h: (child, 0, lax.bitwise_xor(h[0], part) * steps + i)
                ),
            ]
            + [ANY] * len(after),
            out_specs=[pl.BlockSpec((m // pieces, bn), lambda i, h: (0, i))] * pieces,
        ),
        out_shape=[jax.ShapeDtypeStruct((m // pieces, n_half), BF16 if part else F32)] * pieces,
        compiler_params=params(),
        cost_estimate=cost(2 * m * k * n_half, 2 * k * n_half),
    )(core, x, in_hbm(w), *after)


def held_nn(x, w, core, part, pieces=1, after=()):
    m, k = sum(p.shape[0] for p in x), x[0].shape[1]
    n_half = w.shape[1] // 2
    bn = tile_of(n_half, 512, 384, 256, 128)

    def kernel(half_ref, *refs):
        x_value, w_ref = take_pieces(refs[: len(x)]), refs[len(x)]
        outs = refs[len(x) + 1 + len(after) :]
        base = lax.bitwise_xor(half_ref[0], part) * n_half
        rows = m // pieces
        for start in range(0, n_half, bn):
            cols = pl.ds(pl.multiple_of(base + start, LANES), bn)
            product = lax.dot_general(x_value, w_ref[:, cols], NN, preferred_element_type=F32)
            for i, out in enumerate(outs):
                out[:, start : start + bn] = product[i * rows : (i + 1) * rows].astype(out.dtype)

    return pl.pallas_call(
        kernel,
        in_specs=[SCALARS] + [WHOLE] * (len(x) + 1) + [ANY] * len(after),
        out_specs=[WHOLE] * pieces,
        out_shape=[jax.ShapeDtypeStruct((m // pieces, n_half), BF16 if part else F32)] * pieces,
        compiler_params=params(),
        cost_estimate=cost(2 * m * k * n_half, 2 * k * n_half),
    )(core, *x, in_vmem(w), *after)


def held_nt(mine, other, w, core, chunk=0, chunks=1, pieces=1, bring=None, after=()):
    m = sum(x.shape[0] for x in mine)
    k_half = mine[0].shape[1]
    u = w.shape[0] // chunks
    bu = tile_of(u, 512, 384, 256, 128)
    first = chunk * u
    extra = [] if bring is None else [in_hbm(bring[0])]

    def kernel(half_ref, *refs):
        at = len(mine) + len(other)
        a, b, w_ref = take_pieces(refs[: len(mine)]), take_pieces(refs[len(mine) : at]), refs[at]
        outs = refs[at + 1 + len(extra) + len(after) :]
        outs, sem = outs[:-1], outs[-1]
        if extra:
            brought = pltpu.make_async_copy(refs[at + 1].at[bring[1]], outs[-1], sem)
            brought.start()
            outs = outs[:-1]
        low = half_ref[0] == 0
        left, right = jnp.where(low, a, b), jnp.where(low, b, a)
        rows = m // pieces
        for start in range(0, u, bu):
            at = slice(first + start, first + start + bu)
            total = lax.dot_general(left, w_ref[at, :k_half], NT, preferred_element_type=F32)
            total += lax.dot_general(right, w_ref[at, k_half:], NT, preferred_element_type=F32)
            for i, out in enumerate(outs):
                out[:, start : start + bu] = total[i * rows : (i + 1) * rows].astype(out.dtype)
        if extra:
            brought.wait()

    shapes = [jax.ShapeDtypeStruct((m // pieces, u), BF16)] * pieces
    if extra:
        shapes.append(pltpu.VMEM(bring[0].shape[1:], bring[0].dtype))
    return pl.pallas_call(
        kernel,
        in_specs=[SCALARS]
        + [WHOLE] * (len(mine) + len(other) + 1)
        + [IN_HBM] * len(extra)
        + [ANY] * len(after),
        out_specs=[WHOLE] * len(shapes),
        out_shape=shapes,
        scratch_shapes=[pltpu.SemaphoreType.DMA],
        compiler_params=params(),
        cost_estimate=cost(4 * m * k_half * u, 4 * k_half * u),
    )(core, *mine, *other, in_vmem(w), *extra, *after)


def spread_kernel(row_ref, map_ref, *rest):
    o_ref = rest[-1]
    u = map_ref.shape[2]
    step = tile_of(u, LANES)
    for start in range(0, u, step):
        row = map_ref[0, :, start : start + step]
        o_ref[0, start : start + step, :] = jnp.broadcast_to(row, (LANES, step)).T.astype(I16)


def spread(maps, row, u, after=()):
    kids = maps.shape[0]
    return pl.pallas_call(
        spread_kernel,
        grid_spec=pltpu.PrefetchScalarGridSpec(
            num_scalar_prefetch=1,
            grid=(kids,),
            in_specs=[pl.BlockSpec((1, 1, u), lambda k, r: (k, 0, r[0]))] + [ANY] * len(after),
            out_specs=pl.BlockSpec((1, u, LANES), lambda k, r: (k, 0, 0)),
        ),
        out_shape=jax.ShapeDtypeStruct((kids, u, LANES), I16),
        compiler_params=params(),
        cost_estimate=cost(kids * u * LANES, 2 * kids * u * LANES),
    )(row, maps, *after)


def store_in_order(order_ref, chunk, store, value):
    for i in range(value.shape[0] // chunk):
        store(
            pl.ds(pl.multiple_of(lax.bitwise_xor(order_ref[0], i) * chunk, chunk), chunk),
            value[i * chunk : (i + 1) * chunk],
        )


def scatter_kernel(block_rows, tile, odd, chunk, *refs):
    row_ref, order_ref, map_ref, upd_ref, *rest = refs
    o_ref = rest[-1]
    j, t = pl.program_id(0), pl.program_id(1)
    dest = lax.bitwise_xor(row_ref[0], 2 * j + odd)
    first = (dest * block_rows + t * tile).astype(I16)
    local = map_ref[0] - first
    u = local.shape[0]
    sub = tile_of(tile, 256, 128)
    upd = upd_ref[...]
    for start in range(0, tile, sub):
        wide = jnp.concatenate([local] * (sub // LANES), axis=1)
        row_ids = lax.broadcasted_iota(I16, (u, sub), 1) + jnp.int16(start)
        hot = jnp.where(row_ids == wide, BF16(1), BF16(0))
        total = lax.dot_general(upd, hot, NN, preferred_element_type=F32)
        if len(rest) == 2:
            at = slice(start, start + sub)
            before = rest[0]

            def store(ds, value, at=at, before=before):
                o_ref[0, ds, at] = (value + before[0, ds, at].astype(F32)).astype(o_ref.dtype)

        else:
            at = slice(start, start + sub)

            def store(ds, value, at=at):
                o_ref[0, ds, at] = value.astype(o_ref.dtype)

        store_in_order(order_ref, chunk, store, total)


def scatter(upd, spread_maps, child, row, order, rows_count, block_rows, odd, before):
    m, u = upd.shape
    tile = tile_of(block_rows, 768, 512, 384, 256, 128)
    count = rows_count // 2
    chunk = m // order[1]
    block = pl.BlockSpec((1, m, tile), lambda j, t, r, o: (j, 0, t))
    in_specs = [
        pl.BlockSpec((1, u, LANES), lambda j, t, r, o: (child, 0, 0)),
        pl.BlockSpec((m, u), lambda j, t, r, o: (0, 0)),
    ]
    args = [spread_maps, upd]
    if before is not None:
        in_specs.append(block)
        args.append(before)
    return pl.pallas_call(
        functools.partial(scatter_kernel, block_rows, tile, odd, chunk),
        grid_spec=pltpu.PrefetchScalarGridSpec(
            num_scalar_prefetch=2,
            grid=(count, block_rows // tile),
            in_specs=in_specs,
            out_specs=block,
        ),
        out_shape=jax.ShapeDtypeStruct((count, m, block_rows), BF16),
        compiler_params=params(),
        cost_estimate=cost(2 * m * u * count * block_rows, 4 * m * count * block_rows),
    )(row, order[0], *args)


def gather_kernel(block_rows, tile, which, counts, chunk, added, steps, bring, row_ref, order_ref, map_ref, *rest):
    rest, sem = rest[:-1], rest[-1]
    if bring is not None:
        source, target = rest[-3 - bring[1]], rest[-1]
        rest = rest[:-1]
        brought = pltpu.make_async_copy(source.at[bring[0]], target, sem)
        pl.when(pl.program_id(0) == 0)(brought.start)
    o_ref = rest[-1]
    slot_map = map_ref[0]
    total, at = None, 0
    for j, count in zip(which, counts):
        pieces = rest[at : at + count]
        at += count
        first = lax.bitwise_xor(row_ref[0], j) * block_rows
        for start in range(0, block_rows, tile):
            local = (slot_map - (first + start)).astype(I16)
            row_ids = lax.broadcasted_iota(I16, (tile, slot_map.shape[1]), 0)
            hot = jnp.where(row_ids == local, BF16(1), BF16(0))
            block = [p[:, start : start + tile] for p in pieces]
            block = block[0] if count == 1 else jnp.concatenate(block, axis=0)
            term = lax.dot_general(block, hot, NN, preferred_element_type=F32)
            total = term if total is None else total + term

    def store(ds, value):
        if added:
            value = value + rest[at][ds, :].astype(F32)
        o_ref[ds, :] = value.astype(o_ref.dtype)

    store_in_order(order_ref, chunk, store, total)
    if bring is not None:
        pl.when(pl.program_id(0) == steps - 1)(brought.wait)


def gather(blocks, which, maps, u, child, row, order, before, bring=None, after=()):
    m = sum(p.shape[0] for p in blocks[0])
    block_rows = blocks[0][0].shape[1]
    tile = tile_of(block_rows, 512, 384, 256, 128)
    bu = tile_of(u, 512, 384, 256, 128)
    chunk = m // order[1]
    counts = [len(b) for b in blocks]
    steps = u // bu
    in_specs = [pl.BlockSpec((1, 1, bu), lambda i, r, o: (child, 0, r[0] * steps + i))]
    args = [maps]
    for p in (p for b in blocks for p in b):
        in_specs.append(pl.BlockSpec(p.shape, lambda i, r, o: (0, 0)))
        args.append(p)
    out_block = pl.BlockSpec((m, bu), lambda i, r, o: (0, i))
    if before is not None:
        in_specs.append(out_block)
        args.append(before)
    if bring is not None:
        in_specs.append(IN_HBM)
        args.append(in_hbm(bring[0]))
    in_specs += [ANY] * len(after)
    shapes, out_specs = [jax.ShapeDtypeStruct((m, u), BF16)], [out_block]
    if bring is not None:
        shapes.append(pltpu.VMEM(bring[0].shape[1:], bring[0].dtype))
        out_specs.append(WHOLE)
    return pl.pallas_call(
        functools.partial(
            gather_kernel, block_rows,
            tile,
            which,
            counts,
            chunk,
            before is not None,
            steps,
            None if bring is None else (bring[1], len(after)),
        ),
        grid_spec=pltpu.PrefetchScalarGridSpec(
            num_scalar_prefetch=2,
            grid=(steps,),
            in_specs=in_specs,
            out_specs=out_specs,
            scratch_shapes=[pltpu.SemaphoreType.DMA],
        ),
        out_shape=shapes,
        compiler_params=params(),
        cost_estimate=cost(
            2 * m * u * len(blocks) * block_rows, 2 * m * len(blocks) * block_rows
        ),
    )(row, order[0], *args, *after)


def finish(held, kids, child, chunk, chunks, terms):
    m, n = terms[0].shape
    place = pl.BlockSpec((1, m, n), lambda i: (child, 0, chunk))
    whole = pl.BlockSpec((m, n), lambda i: (0, 0))

    def kernel(*refs):
        total = refs[0][...].astype(F32)
        for ref in refs[1 : len(terms)]:
            total += ref[...].astype(F32)
        refs[-2][0] = total
        refs[-1][...] = jnp.zeros_like(refs[-1])

    extra = () if held is None else (in_hbm(held),)
    return pl.pallas_call(
        kernel,
        grid=(1,),
        in_specs=[whole] * len(terms) + [ANY] * len(extra),
        out_specs=[place, pl.BlockSpec(TOKEN.shape, lambda i: (0, 0))],
        out_shape=[pltpu.HBM((kids, m, n * chunks), F32), TOKEN],
        input_output_aliases={len(terms): 0} if extra else {},
        compiler_params=params(),
        cost_estimate=cost(m * n, 8 * m * n),
    )(*terms, *extra)


def reorder(pieces, order):
    m, n = sum(p.shape[0] for p in pieces), pieces[0].shape[1]
    chunk = m // order[1]

    def kernel(order_ref, *refs):
        *inputs, o_ref, token_ref = refs

        def store(ds, value):
            o_ref[ds, :] = value

        store_in_order(order_ref, chunk, store, take_pieces(inputs).astype(F32))
        token_ref[...] = jnp.zeros_like(token_ref)

    return pl.pallas_call(
        kernel,
        in_specs=[SCALARS] + [WHOLE] * len(pieces),
        out_specs=[WHOLE, WHOLE],
        out_shape=[jax.ShapeDtypeStruct((m, n), F32), TOKEN],
        compiler_params=params(),
        cost_estimate=cost(m * n, 6 * m * n),
    )(order[0], *pieces)


def join(terms, signs, after=(), wide=True, narrow=1):
    m = sum(x.shape[0] for x in terms[0])
    n = terms[0][0].shape[1]
    counts = [len(t) for t in terms]

    def kernel(*refs):
        outs = refs[sum(counts) + len(after) :]
        total, at = None, 0
        for count, sign in zip(counts, signs):
            value = take_pieces(refs[at : at + count]).astype(F32)
            at += count
            value = value if sign > 0 else -value
            total = value if total is None else total + value
        if wide:
            outs[0][...] = total
            outs = outs[1:]
        if narrow:
            put_pieces(outs, total)

    shapes = [jax.ShapeDtypeStruct((m, n), F32)] if wide else []
    shapes += [jax.ShapeDtypeStruct((m // narrow, n), BF16)] * narrow if narrow else []
    outs = pl.pallas_call(
        kernel,
        in_specs=[WHOLE] * sum(counts) + [ANY] * len(after),
        out_specs=[WHOLE] * len(shapes),
        out_shape=shapes,
        compiler_params=params(),
        cost_estimate=cost(m * n, 12 * m * n),
    )(*[x for t in terms for x in t], *after)
    return (outs[0] if wide else None), (outs[1:] if wide else outs)


def call_whole(kernel, args, shapes, scalars=(), after=()):
    def body(*refs):
        count = len(scalars) + len(args)
        kernel(*refs[:count], *refs[count + len(after) :])

    return pl.pallas_call(
        body,
        in_specs=[SCALARS] * len(scalars) + [WHOLE] * len(args) + [ANY] * len(after),
        out_specs=[WHOLE] * len(shapes),
        out_shape=[jax.ShapeDtypeStruct(*s) for s in shapes],
        compiler_params=params(),
        cost_estimate=cost(args[0].size, 8 * args[0].size),
    )(*scalars, *args, *after)


def cut_core_sum(kept, got):
    _, m, n = kept.shape
    half, cut = m // 2, n // 2

    def kernel(kept_ref, got_ref, left_ref, left_away, right_ref, right_away):
        for j in range(2):
            left = kept_ref[j, :, :cut].astype(F32) + got_ref[j, :, :cut].astype(F32)
            left_ref[j * half : (j + 1) * half] = left[:half]
            left_away[j * half : (j + 1) * half] = left[half:].astype(BF16)
            right = kept_ref[j, :, cut:].astype(F32) + got_ref[j, :, cut:].astype(F32)
            if j == 0:
                right_ref[...] = right
            else:
                right_away[...] = right.astype(BF16)

    shape = (m, cut)
    return call_whole(
        kernel, (kept, got), [(shape, F32), (shape, BF16), (shape, F32), (shape, BF16)]
    )


def cut_rows(kept, got):
    m, n = kept.shape

    def kernel(kept_ref, got_ref, first, second):
        total = kept_ref[...] + got_ref[...].astype(F32)
        first[...] = total[: m // 2]
        second[...] = total[m // 2 :].astype(BF16)

    return call_whole(kernel, (kept, got), [((m // 2, n), F32), ((m // 2, n), BF16)])


def cut_cases(left, left_got, right, right_got, count):
    m, n = left.shape
    piece = m // count

    def kernel(a, b, c, d, *outs):
        sums = a[...] + b[...].astype(F32), c[...] + d[...].astype(F32)
        for i, out in enumerate(outs):
            for at, total in enumerate(sums):
                rows = total[i * piece : (i + 1) * piece]
                out[:, at * n : (at + 1) * n] = rows.astype(out.dtype)

    shapes = [((piece, 2 * n), BF16 if i else F32) for i in range(count)]
    return call_whole(kernel, (left, left_got, right, right_got), shapes)


def residual_of(loads, first, terms, after):
    piece, n = terms[0].shape

    def kernel(first_ref, loads_ref, *refs):
        rows = pl.ds(pl.multiple_of(first_ref[0] * piece, piece), piece)
        total = refs[0][...].astype(F32)
        for ref in refs[1:-1]:
            total += ref[...].astype(F32)
        refs[-1][...] = (loads_ref[rows, :].astype(F32) - total).astype(BF16)

    return call_whole(kernel, (loads, *terms), [((piece, n), BF16)], (first,), after)[0]


def swap(x, axis, bit, size):
    return lax.ppermute(x, axis, [(i, i ^ bit) for i in range(size)])


def add(x, y):
    return x.astype(F32) + y.astype(F32)


def bits(size):
    return [1 << b for b in range(size.bit_length() - 1)]


def on_device(sizes, child_loads, child_inverse, child_panel, child_map, root_loads, root_inverse):
    leafs, rows, cols = sizes
    kids = child_loads.shape[0]
    case_count, root_rows = root_loads.shape
    leaf, row, col = (lax.axis_index(a).astype(jnp.int32) for a in ("leaf", "row", "col"))
    core = lax.bitwise_and(row, 1)[None]
    row_1 = row[None]
    root_w = root_inverse[None]
    piece = case_count // (leafs * cols)
    wide = rows == 4 and cols == 2 and piece % 16 == 0 and root_rows % 256 == 0

    def to_row(x, bit):
        return swap(x, "row", bit, rows)

    def to_col(x, bit=1):
        return swap(x, "col", bit, cols)

    def to_leaf(x, j):
        return swap(x, "leaf", j, leafs)

    def pieces_of(k, m=case_count):
        return 4 if k and m % 64 == 0 else 1

    def core_sum(kept, sent):
        total, narrow = join([[kept], [to_row(x, 1) for x in sent]], (1, 1))
        return total, narrow[0]

    def row_end(total, narrow, after=(), base=None, wide=True, pieces=1):
        steps = bits(rows)[1:]
        for at, bit in enumerate(steps):
            last = at == len(steps) - 1
            terms, signs = [[total], [to_row(narrow, bit)]], (1, 1)
            if last and base is not None:
                terms, signs = [base, *terms], (1, -1, -1)
            total, out = join(
                terms, signs, after, wide or not last, pieces if last else 1
            )
            narrow = out[0]
        return total, out

    def halves(rounded):
        return rounded, [to_row(x, 1) for x in rounded]

    slot_rows = child_panel.shape[1]
    maps = child_map.reshape(kids, 1, child_map.shape[1])

    share = (col * leafs + leaf)[None]
    order = (share, cols * leafs) if wide else (jnp.zeros((1,), jnp.int32), 1)

    begun = []
    after = ()
    for k in range(kids):
        sent = nn(child_loads, child_inverse, k, core, 1, pieces_of(k), after)
        (kept,) = nn(child_loads, child_inverse, k, core, 0, 1, sent[:1])
        begun.append(core_sum(kept, sent))
        after = begun[k][1:]
    spread_maps = spread(maps, row_1, slot_rows, after)
    after = (spread_maps,)
    forward = []
    sent = kept = None
    for k in range(kids):
        after = after if k == 0 else (sent,)
        _, rounded = row_end(*begun[k], after, wide=False, pieces=pieces_of(k == 0))
        forward.append(rounded)
        if k == 0:
            panel, _ = preload(child_panel, 0, rounded)
        bring = (child_panel, k + 1) if k < kids - 1 else None
        upd, *brought = held_nt(*halves(rounded), panel, core, bring=bring)
        panel = brought[0] if brought else None
        sent = scatter(upd, spread_maps, k, row_1, order, rows, root_rows, 1, sent)
        kept = scatter(upd, spread_maps, k, row_1, order, rows, root_rows, 0, kept)

    if wide:
        left, left_away, right, right_away = cut_core_sum(kept, to_row(sent, 1))
        left_got, right_got = to_col(left_away), to_row(right_away, 2)
        left, left_away = cut_rows(left, left_got)
        right, right_away = cut_rows(right, right_got)
        mine, *shares = cut_cases(
            left, to_row(left_away, 2), right, to_col(right_away), leafs
        )
        root_held, token = preload(root_w, 0, shares)
        terms = [mine] + [to_leaf(x, j + 1) for j, x in enumerate(shares)]
        residual = residual_of(root_loads, share, terms, (token,))
        residual = [residual, to_col(residual)]
    else:
        total = add(kept, to_row(sent, 1))
        for bit in bits(rows)[1:]:
            total = add(total[0::2], to_row(total[1::2].astype(BF16), bit))
        total = total[0]
        chunk = case_count // leafs

        def cases_of(x, j):
            return lax.dynamic_slice_in_dim(x, lax.bitwise_xor(leaf, j) * chunk, chunk, 0)

        narrow = total.astype(BF16)
        mine_cases = cases_of(total, 0)
        for j in range(1, leafs):
            mine_cases = add(mine_cases, to_leaf(cases_of(narrow, j), j))
        for bit in bits(cols):
            narrow = mine_cases.astype(BF16)
            mine_cases = add(narrow, to_col(narrow, bit))
        residual = [(cases_of(root_loads, 0).astype(F32) - mine_cases).astype(BF16)]
        root_held, _ = preload(root_w, 0, (kept,))

    sent = held_nn(residual, root_held, core, 1)
    kept = held_nn(residual, root_held, core, 0, 1, sent)
    begun = core_sum(kept[0], sent)
    *panels, token = preload(child_panel, 0, begun[1:])
    _, root_forward = row_end(*begun, (token,), wide=False)
    *part, panel = held_nt(
        *halves(root_forward),
        root_held,
        core,
        pieces=2 if wide else 1,
        bring=(child_panel, kids - 1),
    )
    panels += [preload(child_panel, k, part)[0] for k in range(1, kids - 1)] + [panel]

    picked = [None] * kids
    inverses = []
    if wide:
        _, (part,) = join([[part[0]], [to_col(part[1])]], (1, 1), (), False)
        shares = [part] + [to_leaf(part, j) for j in range(1, leafs)]
        _, (held,) = join([shares], (1,), (), False)
        brought = [preload(child_inverse, k, (held,)) for k in range(kids - 1)]
        inverses = [b[0] for b in brought]
        tokens = tuple(b[1] for b in brought)
        beside, across = to_col(held), to_row(held, 2)
        cut = held.shape[0] // 2
        _, near = join([[held, beside]], (1,), tokens, False, 4)
        near_other = [to_row(x, 1) for x in near]
        rest = [to_col(across[:cut]), to_row(beside[cut:], 2)]
        for k in range(kids):
            (picked[k],) = gather(
                [near, near_other], [0, 1], maps, slot_rows, k, row_1, order, None, None, (across,)
            )
        _, far = join([[across, *rest]], (1,), tuple(picked), False)
        far_other = [to_row(x, 1) for x in far]
        root_solution, token = reorder(near, order)
        last_blocks, last_at = [far, far_other], [2, 3]
    else:
        (part,) = part
        inverses = [preload(child_inverse, k, (part,))[0] for k in range(kids - 1)]
        for bit in bits(cols):
            part = add(part, to_col(part, bit)).astype(BF16)
        own = jnp.zeros((case_count, root_rows), BF16)
        for j in range(leafs):
            got = part if j == 0 else to_leaf(part, j)
            own = lax.dynamic_update_slice_in_dim(
                own, got, lax.bitwise_xor(leaf, j) * (case_count // leafs), 0
            )
        root_solution = own.astype(F32)
        groups = [own]
        for bit in [1, *bits(rows)[1:]]:
            got = to_row(jnp.stack(groups), bit)
            groups += [got[i] for i in range(len(groups))]
        last_blocks, last_at = [[g] for g in groups], list(range(rows))

    begun = []
    after = ()
    for k in range(kids):
        bring = (child_inverse, k) if k == kids - 1 else None
        full, *brought = gather(
            last_blocks, last_at, maps, slot_rows, k, row_1, order, picked[k], bring, after
        )
        inverses += brought
        sent = held_nn([full], panels[k], core, 1, pieces_of(k))
        kept = held_nn([full], panels[k], core, 0, 1, sent[:1])
        begun.append(core_sum(kept[0], sent))
        after = begun[k][1:]
    solved = first = None
    chunks = 2 if slot_rows % 256 == 0 else 1
    after = (token, *after)
    for k in range(kids):
        _, rounded = row_end(*begun[k], after, forward[k], False, pieces_of(1))
        pair = halves(rounded)
        after = ()
        for at in range(chunks):
            ready = (first,) if k and at else ()
            (out,) = held_nt(*pair, inverses[k], core, at, chunks, after=ready)
            after += (out,)
            terms = [out, to_col(out)]
            for bit in bits(cols)[1:]:
                out = add(*terms).astype(BF16)
                terms = [out, to_col(out, bit)]
            solved, done = finish(solved, kids, k, at, chunks, terms)
            first = done if first is None else first
    return (solved, root_solution)


def solution(mesh):
    sizes = tuple(mesh.shape[a] for a in ("leaf", "row", "col"))
    in_specs = (
        P("leaf", None, "row"),
        P("leaf", "row", "col"),
        P("leaf", "row", "col"),
        P("leaf", None),
        P(None, "row"),
        P("row", "col"),
    )
    out_specs = (P("leaf", None, "row"), P(None, "row"))
    return jax.shard_map(
        functools.partial(on_device, sizes),
        mesh=mesh,
        in_specs=in_specs,
        out_specs=out_specs,
        check_vma=False,
    )
```

```python
import functools

import jax
import jax.numpy as jnp
from jax import lax
from jax.experimental import pallas as pl
from jax.experimental.pallas import tpu as pltpu
from jax.sharding import PartitionSpec as P

BF16 = jnp.bfloat16
F32 = jnp.float32
I16 = jnp.int16
NN = (((1,), (0,)), ((), ()))
NT = (((1,), (1,)), ((), ()))
LANES = 128
ANY = pl.BlockSpec(memory_space=pl.ANY)
WHOLE = pl.BlockSpec(memory_space=pltpu.VMEM)
SCALARS = pl.BlockSpec(memory_space=pltpu.SMEM)
IN_HBM = pl.BlockSpec(memory_space=pltpu.HBM)


def tile_of(extent, *sizes):
    for size in sizes:
        if extent % size == 0:
            return size
    return extent


def params():
    return pltpu.CompilerParams(vmem_limit_bytes=10 * 1024 * 1024)


def cost(flops, nbytes):
    return pl.CostEstimate(flops=flops // 64, bytes_accessed=nbytes // 64, transcendentals=0)


def in_hbm(w):
    return pltpu.with_memory_space_constraint(w, pltpu.HBM)


def in_vmem(w):
    return pltpu.with_memory_space_constraint(w, pltpu.VMEM)


TOKEN = jax.ShapeDtypeStruct((8, LANES), F32)


def preload_kernel(child, w_ref, *rest):
    o_ref, token_ref, sem = rest[-3:]
    copy = pltpu.make_async_copy(w_ref.at[child], o_ref, sem)
    copy.start()
    token_ref[...] = jnp.zeros_like(token_ref)
    copy.wait()


def preload(w, child, after=()):
    return pl.pallas_call(
        functools.partial(preload_kernel, child),
        in_specs=[pl.BlockSpec(memory_space=pltpu.HBM)] + [ANY] * len(after),
        out_specs=[WHOLE, WHOLE],
        out_shape=[pltpu.VMEM(w.shape[1:], w.dtype), TOKEN],
        scratch_shapes=[pltpu.SemaphoreType.DMA],
        compiler_params=params(),
        cost_estimate=cost(0, w[0].size * 2),
    )(in_hbm(w), *after)


def put_pieces(refs, value):
    rows = value.shape[0] // len(refs)
    for i, ref in enumerate(refs):
        ref[...] = value[i * rows : (i + 1) * rows].astype(ref.dtype)


def take_pieces(refs):
    return refs[0][...] if len(refs) == 1 else jnp.concatenate([r[...] for r in refs], axis=0)


def nn_kernel(half_ref, x_ref, w_ref, *outs):
    x = x_ref[0] if len(x_ref.shape) == 3 else x_ref[...]
    product = lax.dot_general(x, w_ref[0], NN, preferred_element_type=F32)
    put_pieces(outs, product)


def nn(x, w, child, core, part, pieces=1, after=()):
    m, k = x.shape[-2:]
    n_half = w.shape[2] // 2
    bn = tile_of(n_half, 768, 512, 384, 256, 128)
    steps = n_half // bn
    if x.ndim == 3:
        x_spec = pl.BlockSpec((1, m, k), lambda i, h: (child, 0, 0))
        x = in_hbm(x)
    else:
        x_spec = pl.BlockSpec((m, k), lambda i, h: (0, 0))

    def kernel(half_ref, x_ref, w_ref, *rest):
        nn_kernel(half_ref, x_ref, w_ref, *rest[len(after) :])

    return pl.pallas_call(
        kernel,
        grid_spec=pltpu.PrefetchScalarGridSpec(
            num_scalar_prefetch=1,
            grid=(steps,),
            in_specs=[
                x_spec,
                pl.BlockSpec(
                    (1, k, bn), lambda i, h: (child, 0, lax.bitwise_xor(h[0], part) * steps + i)
                ),
            ]
            + [ANY] * len(after),
            out_specs=[pl.BlockSpec((m // pieces, bn), lambda i, h: (0, i))] * pieces,
        ),
        out_shape=[jax.ShapeDtypeStruct((m // pieces, n_half), BF16 if part else F32)] * pieces,
        compiler_params=params(),
        cost_estimate=cost(2 * m * k * n_half, 2 * k * n_half),
    )(core, x, in_hbm(w), *after)


def held_nn(x, w, core, part, pieces=1, after=()):
    m, k = sum(p.shape[0] for p in x), x[0].shape[1]
    n_half = w.shape[1] // 2
    bn = tile_of(n_half, 512, 384, 256, 128)

    def kernel(half_ref, *refs):
        x_value, w_ref = take_pieces(refs[: len(x)]), refs[len(x)]
        outs = refs[len(x) + 1 + len(after) :]
        base = lax.bitwise_xor(half_ref[0], part) * n_half
        rows = m // pieces
        for start in range(0, n_half, bn):
            cols = pl.ds(pl.multiple_of(base + start, LANES), bn)
            product = lax.dot_general(x_value, w_ref[:, cols], NN, preferred_element_type=F32)
            for i, out in enumerate(outs):
                out[:, start : start + bn] = product[i * rows : (i + 1) * rows].astype(out.dtype)

    return pl.pallas_call(
        kernel,
        in_specs=[SCALARS] + [WHOLE] * (len(x) + 1) + [ANY] * len(after),
        out_specs=[WHOLE] * pieces,
        out_shape=[jax.ShapeDtypeStruct((m // pieces, n_half), BF16 if part else F32)] * pieces,
        compiler_params=params(),
        cost_estimate=cost(2 * m * k * n_half, 2 * k * n_half),
    )(core, *x, in_vmem(w), *after)


def held_nt(mine, other, w, core, chunk=0, chunks=1, pieces=1, bring=None, after=()):
    m = sum(x.shape[0] for x in mine)
    k_half = mine[0].shape[1]
    u = w.shape[0] // chunks
    bu = tile_of(u, 512, 384, 256, 128)
    first = chunk * u
    extra = [] if bring is None else [in_hbm(bring[0])]

    def kernel(half_ref, *refs):
        at = len(mine) + len(other)
        a, b, w_ref = take_pieces(refs[: len(mine)]), take_pieces(refs[len(mine) : at]), refs[at]
        outs = refs[at + 1 + len(extra) + len(after) :]
        outs, sem = outs[:-1], outs[-1]
        if extra:
            brought = pltpu.make_async_copy(refs[at + 1].at[bring[1]], outs[-1], sem)
            brought.start()
            outs = outs[:-1]
        low = half_ref[0] == 0
        left, right = jnp.where(low, a, b), jnp.where(low, b, a)
        rows = m // pieces
        for start in range(0, u, bu):
            at = slice(first + start, first + start + bu)
            total = lax.dot_general(left, w_ref[at, :k_half], NT, preferred_element_type=F32)
            total += lax.dot_general(right, w_ref[at, k_half:], NT, preferred_element_type=F32)
            for i, out in enumerate(outs):
                out[:, start : start + bu] = total[i * rows : (i + 1) * rows].astype(out.dtype)
        if extra:
            brought.wait()

    shapes = [jax.ShapeDtypeStruct((m // pieces, u), BF16)] * pieces
    if extra:
        shapes.append(pltpu.VMEM(bring[0].shape[1:], bring[0].dtype))
    return pl.pallas_call(
        kernel,
        in_specs=[SCALARS]
        + [WHOLE] * (len(mine) + len(other) + 1)
        + [IN_HBM] * len(extra)
        + [ANY] * len(after),
        out_specs=[WHOLE] * len(shapes),
        out_shape=shapes,
        scratch_shapes=[pltpu.SemaphoreType.DMA],
        compiler_params=params(),
        cost_estimate=cost(4 * m * k_half * u, 4 * k_half * u),
    )(core, *mine, *other, in_vmem(w), *extra, *after)


def spread_kernel(row_ref, map_ref, *rest):
    o_ref = rest[-1]
    u = map_ref.shape[2]
    step = tile_of(u, LANES)
    for start in range(0, u, step):
        row = map_ref[0, :, start : start + step]
        o_ref[0, start : start + step, :] = jnp.broadcast_to(row, (LANES, step)).T.astype(I16)


def spread(maps, row, u, after=()):
    kids = maps.shape[0]
    return pl.pallas_call(
        spread_kernel,
        grid_spec=pltpu.PrefetchScalarGridSpec(
            num_scalar_prefetch=1,
            grid=(kids,),
            in_specs=[pl.BlockSpec((1, 1, u), lambda k, r: (k, 0, r[0]))] + [ANY] * len(after),
            out_specs=pl.BlockSpec((1, u, LANES), lambda k, r: (k, 0, 0)),
        ),
        out_shape=jax.ShapeDtypeStruct((kids, u, LANES), I16),
        compiler_params=params(),
        cost_estimate=cost(kids * u * LANES, 2 * kids * u * LANES),
    )(row, maps, *after)


def store_in_order(order_ref, chunk, store, value):
    for i in range(value.shape[0] // chunk):
        store(
            pl.ds(pl.multiple_of(lax.bitwise_xor(order_ref[0], i) * chunk, chunk), chunk),
            value[i * chunk : (i + 1) * chunk],
        )


def scatter_kernel(block_rows, tile, odd, chunk, *refs):
    row_ref, order_ref, map_ref, upd_ref, *rest = refs
    o_ref = rest[-1]
    j, t = pl.program_id(0), pl.program_id(1)
    dest = lax.bitwise_xor(row_ref[0], 2 * j + odd)
    first = (dest * block_rows + t * tile).astype(I16)
    local = map_ref[0] - first
    u = local.shape[0]
    sub = tile_of(tile, 256, 128)
    upd = upd_ref[...]
    for start in range(0, tile, sub):
        wide = jnp.concatenate([local] * (sub // LANES), axis=1)
        row_ids = lax.broadcasted_iota(I16, (u, sub), 1) + jnp.int16(start)
        hot = jnp.where(row_ids == wide, BF16(1), BF16(0))
        total = lax.dot_general(upd, hot, NN, preferred_element_type=F32)
        if len(rest) == 2:
            at = slice(start, start + sub)
            before = rest[0]

            def store(ds, value, at=at, before=before):
                o_ref[0, ds, at] = (value + before[0, ds, at].astype(F32)).astype(o_ref.dtype)

        else:
            at = slice(start, start + sub)

            def store(ds, value, at=at):
                o_ref[0, ds, at] = value.astype(o_ref.dtype)

        store_in_order(order_ref, chunk, store, total)


def scatter(upd, spread_maps, child, row, order, rows_count, block_rows, odd, before):
    m, u = upd.shape
    tile = tile_of(block_rows, 768, 512, 384, 256, 128)
    count = rows_count // 2
    chunk = m // order[1]
    block = pl.BlockSpec((1, m, tile), lambda j, t, r, o: (j, 0, t))
    in_specs = [
        pl.BlockSpec((1, u, LANES), lambda j, t, r, o: (child, 0, 0)),
        pl.BlockSpec((m, u), lambda j, t, r, o: (0, 0)),
    ]
    args = [spread_maps, upd]
    if before is not None:
        in_specs.append(block)
        args.append(before)
    return pl.pallas_call(
        functools.partial(scatter_kernel, block_rows, tile, odd, chunk),
        grid_spec=pltpu.PrefetchScalarGridSpec(
            num_scalar_prefetch=2,
            grid=(count, block_rows // tile),
            in_specs=in_specs,
            out_specs=block,
        ),
        out_shape=jax.ShapeDtypeStruct((count, m, block_rows), BF16),
        compiler_params=params(),
        cost_estimate=cost(2 * m * u * count * block_rows, 4 * m * count * block_rows),
    )(row, order[0], *args)


def gather_kernel(block_rows, tile, which, counts, chunk, added, steps, bring, row_ref, order_ref, map_ref, *rest):
    rest, sem = rest[:-1], rest[-1]
    if bring is not None:
        source, target = rest[-3 - bring[1]], rest[-1]
        rest = rest[:-1]
        brought = pltpu.make_async_copy(source.at[bring[0]], target, sem)
        pl.when(pl.program_id(0) == 0)(brought.start)
    o_ref = rest[-1]
    slot_map = map_ref[0]
    total, at = None, 0
    for j, count in zip(which, counts):
        pieces = rest[at : at + count]
        at += count
        first = lax.bitwise_xor(row_ref[0], j) * block_rows
        for start in range(0, block_rows, tile):
            local = (slot_map - (first + start)).astype(I16)
            row_ids = lax.broadcasted_iota(I16, (tile, slot_map.shape[1]), 0)
            hot = jnp.where(row_ids == local, BF16(1), BF16(0))
            block = [p[:, start : start + tile] for p in pieces]
            block = block[0] if count == 1 else jnp.concatenate(block, axis=0)
            term = lax.dot_general(block, hot, NN, preferred_element_type=F32)
            total = term if total is None else total + term

    def store(ds, value):
        if added:
            value = value + rest[at][ds, :].astype(F32)
        o_ref[ds, :] = value.astype(o_ref.dtype)

    store_in_order(order_ref, chunk, store, total)
    if bring is not None:
        pl.when(pl.program_id(0) == steps - 1)(brought.wait)


def gather(blocks, which, maps, u, child, row, order, before, bring=None, after=()):
    m = sum(p.shape[0] for p in blocks[0])
    block_rows = blocks[0][0].shape[1]
    tile = tile_of(block_rows, 512, 384, 256, 128)
    bu = tile_of(u, 512, 384, 256, 128)
    chunk = m // order[1]
    counts = [len(b) for b in blocks]
    steps = u // bu
    in_specs = [pl.BlockSpec((1, 1, bu), lambda i, r, o: (child, 0, r[0] * steps + i))]
    args = [maps]
    for p in (p for b in blocks for p in b):
        in_specs.append(pl.BlockSpec(p.shape, lambda i, r, o: (0, 0)))
        args.append(p)
    out_block = pl.BlockSpec((m, bu), lambda i, r, o: (0, i))
    if before is not None:
        in_specs.append(out_block)
        args.append(before)
    if bring is not None:
        in_specs.append(IN_HBM)
        args.append(in_hbm(bring[0]))
    in_specs += [ANY] * len(after)
    shapes, out_specs = [jax.ShapeDtypeStruct((m, u), BF16)], [out_block]
    if bring is not None:
        shapes.append(pltpu.VMEM(bring[0].shape[1:], bring[0].dtype))
        out_specs.append(WHOLE)
    return pl.pallas_call(
        functools.partial(
            gather_kernel, block_rows,
            tile,
            which,
            counts,
            chunk,
            before is not None,
            steps,
            None if bring is None else (bring[1], len(after)),
        ),
        grid_spec=pltpu.PrefetchScalarGridSpec(
            num_scalar_prefetch=2,
            grid=(steps,),
            in_specs=in_specs,
            out_specs=out_specs,
            scratch_shapes=[pltpu.SemaphoreType.DMA],
        ),
        out_shape=shapes,
        compiler_params=params(),
        cost_estimate=cost(
            2 * m * u * len(blocks) * block_rows, 2 * m * len(blocks) * block_rows
        ),
    )(row, order[0], *args, *after)


def finish(held, kids, child, chunk, chunks, terms):
    m, n = terms[0].shape
    place = pl.BlockSpec((1, m, n), lambda i: (child, 0, chunk))
    whole = pl.BlockSpec((m, n), lambda i: (0, 0))

    def kernel(*refs):
        total = refs[0][...].astype(F32)
        for ref in refs[1 : len(terms)]:
            total += ref[...].astype(F32)
        refs[-2][0] = total
        refs[-1][...] = jnp.zeros_like(refs[-1])

    extra = () if held is None else (in_hbm(held),)
    return pl.pallas_call(
        kernel,
        grid=(1,),
        in_specs=[whole] * len(terms) + [ANY] * len(extra),
        out_specs=[place, pl.BlockSpec(TOKEN.shape, lambda i: (0, 0))],
        out_shape=[pltpu.HBM((kids, m, n * chunks), F32), TOKEN],
        input_output_aliases={len(terms): 0} if extra else {},
        compiler_params=params(),
        cost_estimate=cost(m * n, 8 * m * n),
    )(*terms, *extra)


def reorder(pieces, order):
    m, n = sum(p.shape[0] for p in pieces), pieces[0].shape[1]
    chunk = m // order[1]

    def kernel(order_ref, *refs):
        *inputs, o_ref, token_ref = refs

        def store(ds, value):
            o_ref[ds, :] = value

        store_in_order(order_ref, chunk, store, take_pieces(inputs).astype(F32))
        token_ref[...] = jnp.zeros_like(token_ref)

    return pl.pallas_call(
        kernel,
        in_specs=[SCALARS] + [WHOLE] * len(pieces),
        out_specs=[WHOLE, WHOLE],
        out_shape=[jax.ShapeDtypeStruct((m, n), F32), TOKEN],
        compiler_params=params(),
        cost_estimate=cost(m * n, 6 * m * n),
    )(order[0], *pieces)


def join(terms, signs, after=(), wide=True, narrow=1):
    m = sum(x.shape[0] for x in terms[0])
    n = terms[0][0].shape[1]
    counts = [len(t) for t in terms]

    def kernel(*refs):
        outs = refs[sum(counts) + len(after) :]
        total, at = None, 0
        for count, sign in zip(counts, signs):
            value = take_pieces(refs[at : at + count]).astype(F32)
            at += count
            value = value if sign > 0 else -value
            total = value if total is None else total + value
        if wide:
            outs[0][...] = total
            outs = outs[1:]
        if narrow:
            put_pieces(outs, total)

    shapes = [jax.ShapeDtypeStruct((m, n), F32)] if wide else []
    shapes += [jax.ShapeDtypeStruct((m // narrow, n), BF16)] * narrow if narrow else []
    outs = pl.pallas_call(
        kernel,
        in_specs=[WHOLE] * sum(counts) + [ANY] * len(after),
        out_specs=[WHOLE] * len(shapes),
        out_shape=shapes,
        compiler_params=params(),
        cost_estimate=cost(m * n, 12 * m * n),
    )(*[x for t in terms for x in t], *after)
    return (outs[0] if wide else None), (outs[1:] if wide else outs)


def call_whole(kernel, args, shapes, scalars=(), after=()):
    def body(*refs):
        count = len(scalars) + len(args)
        kernel(*refs[:count], *refs[count + len(after) :])

    return pl.pallas_call(
        body,
        in_specs=[SCALARS] * len(scalars) + [WHOLE] * len(args) + [ANY] * len(after),
        out_specs=[WHOLE] * len(shapes),
        out_shape=[jax.ShapeDtypeStruct(*s) for s in shapes],
        compiler_params=params(),
        cost_estimate=cost(args[0].size, 8 * args[0].size),
    )(*scalars, *args, *after)


def cut_core_sum(kept, got):
    _, m, n = kept.shape
    half, cut = m // 2, n // 2

    def kernel(kept_ref, got_ref, left_ref, left_away, right_ref, right_away):
        for j in range(2):
            left = kept_ref[j, :, :cut].astype(F32) + got_ref[j, :, :cut].astype(F32)
            left_ref[j * half : (j + 1) * half] = left[:half]
            left_away[j * half : (j + 1) * half] = left[half:].astype(BF16)
            right = kept_ref[j, :, cut:].astype(F32) + got_ref[j, :, cut:].astype(F32)
            if j == 0:
                right_ref[...] = right
            else:
                right_away[...] = right.astype(BF16)

    shape = (m, cut)
    return call_whole(
        kernel, (kept, got), [(shape, F32), (shape, BF16), (shape, F32), (shape, BF16)]
    )


def cut_rows(kept, got):
    m, n = kept.shape

    def kernel(kept_ref, got_ref, first, second):
        total = kept_ref[...] + got_ref[...].astype(F32)
        first[...] = total[: m // 2]
        second[...] = total[m // 2 :].astype(BF16)

    return call_whole(kernel, (kept, got), [((m // 2, n), F32), ((m // 2, n), BF16)])


def cut_cases(left, left_got, right, right_got, count):
    m, n = left.shape
    piece = m // count

    def kernel(a, b, c, d, *outs):
        sums = a[...] + b[...].astype(F32), c[...] + d[...].astype(F32)
        for i, out in enumerate(outs):
            for at, total in enumerate(sums):
                rows = total[i * piece : (i + 1) * piece]
                out[:, at * n : (at + 1) * n] = rows.astype(out.dtype)

    shapes = [((piece, 2 * n), BF16 if i else F32) for i in range(count)]
    return call_whole(kernel, (left, left_got, right, right_got), shapes)


def residual_of(loads, first, terms, after):
    piece, n = terms[0].shape

    def kernel(first_ref, loads_ref, *refs):
        rows = pl.ds(pl.multiple_of(first_ref[0] * piece, piece), piece)
        total = refs[0][...].astype(F32)
        for ref in refs[1:-1]:
            total += ref[...].astype(F32)
        refs[-1][...] = (loads_ref[rows, :].astype(F32) - total).astype(BF16)

    return call_whole(kernel, (loads, *terms), [((piece, n), BF16)], (first,), after)[0]


def swap(x, axis, bit, size):
    return lax.ppermute(x, axis, [(i, i ^ bit) for i in range(size)])


def add(x, y):
    return x.astype(F32) + y.astype(F32)


def bits(size):
    return [1 << b for b in range(size.bit_length() - 1)]


def on_device(sizes, child_loads, child_inverse, child_panel, child_map, root_loads, root_inverse):
    leafs, rows, cols = sizes
    kids = child_loads.shape[0]
    case_count, root_rows = root_loads.shape
    leaf, row, col = (lax.axis_index(a).astype(jnp.int32) for a in ("leaf", "row", "col"))
    core = lax.bitwise_and(row, 1)[None]
    row_1 = row[None]
    root_w = root_inverse[None]
    piece = case_count // (leafs * cols)
    wide = rows == 4 and cols == 2 and piece % 16 == 0 and root_rows % 256 == 0

    def to_row(x, bit):
        return swap(x, "row", bit, rows)

    def to_col(x, bit=1):
        return swap(x, "col", bit, cols)

    def to_leaf(x, j):
        return swap(x, "leaf", j, leafs)

    def pieces_of(k, m=case_count):
        return 4 if k and m % 64 == 0 else 1

    def core_sum(kept, sent):
        total, narrow = join([[kept], [to_row(x, 1) for x in sent]], (1, 1))
        return total, narrow[0]

    def row_end(total, narrow, after=(), base=None, wide=True, pieces=1):
        steps = bits(rows)[1:]
        for at, bit in enumerate(steps):
            last = at == len(steps) - 1
            terms, signs = [[total], [to_row(narrow, bit)]], (1, 1)
            if last and base is not None:
                terms, signs = [base, *terms], (1, -1, -1)
            total, out = join(
                terms, signs, after, wide or not last, pieces if last else 1
            )
            narrow = out[0]
        return total, out

    def halves(rounded):
        return rounded, [to_row(x, 1) for x in rounded]

    slot_rows = child_panel.shape[1]
    maps = child_map.reshape(kids, 1, child_map.shape[1])

    share = (col * leafs + leaf)[None]
    order = (share, cols * leafs) if wide else (jnp.zeros((1,), jnp.int32), 1)

    begun = []
    after = ()
    for k in range(kids):
        sent = nn(child_loads, child_inverse, k, core, 1, pieces_of(k), after)
        (kept,) = nn(child_loads, child_inverse, k, core, 0, 1, sent[:1])
        begun.append(core_sum(kept, sent))
        after = begun[k][1:]
    spread_maps = spread(maps, row_1, slot_rows, after)
    after = (spread_maps,)
    forward = []
    sent = kept = None
    for k in range(kids):
        after = after if k == 0 else (sent,)
        _, rounded = row_end(*begun[k], after, wide=False, pieces=pieces_of(k == 0))
        forward.append(rounded)
        if k == 0:
            panel, _ = preload(child_panel, 0, rounded)
        bring = (child_panel, k + 1) if k < kids - 1 else None
        ready = () if kept is None else (kept,)
        upd, *brought = held_nt(*halves(rounded), panel, core, bring=bring, after=ready)
        panel = brought[0] if brought else None
        sent = scatter(upd, spread_maps, k, row_1, order, rows, root_rows, 1, sent)
        kept = scatter(upd, spread_maps, k, row_1, order, rows, root_rows, 0, kept)

    if wide:
        left, left_away, right, right_away = cut_core_sum(kept, to_row(sent, 1))
        left_got, right_got = to_col(left_away), to_row(right_away, 2)
        left, left_away = cut_rows(left, left_got)
        right, right_away = cut_rows(right, right_got)
        mine, *shares = cut_cases(
            left, to_row(left_away, 2), right, to_col(right_away), leafs
        )
        root_held, token = preload(root_w, 0, shares)
        terms = [mine] + [to_leaf(x, j + 1) for j, x in enumerate(shares)]
        residual = residual_of(root_loads, share, terms, (token,))
        residual = [residual, to_col(residual)]
    else:
        total = add(kept, to_row(sent, 1))
        for bit in bits(rows)[1:]:
            total = add(total[0::2], to_row(total[1::2].astype(BF16), bit))
        total = total[0]
        chunk = case_count // leafs

        def cases_of(x, j):
            return lax.dynamic_slice_in_dim(x, lax.bitwise_xor(leaf, j) * chunk, chunk, 0)

        narrow = total.astype(BF16)
        mine_cases = cases_of(total, 0)
        for j in range(1, leafs):
            mine_cases = add(mine_cases, to_leaf(cases_of(narrow, j), j))
        for bit in bits(cols):
            narrow = mine_cases.astype(BF16)
            mine_cases = add(narrow, to_col(narrow, bit))
        residual = [(cases_of(root_loads, 0).astype(F32) - mine_cases).astype(BF16)]
        root_held, _ = preload(root_w, 0, (kept,))

    sent = held_nn(residual, root_held, core, 1)
    kept = held_nn(residual, root_held, core, 0, 1, sent)
    begun = core_sum(kept[0], sent)
    *panels, token = preload(child_panel, 0, begun[1:])
    _, root_forward = row_end(*begun, (token,), wide=False)
    part = held_nt(*halves(root_forward), root_held, core, pieces=2 if wide else 1)

    picked = [None] * kids
    inverses = []
    if wide:
        _, (part,) = join([[part[0]], [to_col(part[1])]], (1, 1), (), False)
        shares = [part] + [to_leaf(part, j) for j in range(1, leafs)]
        brought = [preload(child_panel, k, (part,)) for k in range(1, kids)]
        panels += [b[0] for b in brought]
        _, (held,) = join([shares], (1,), tuple(b[1] for b in brought), False)
        brought = [preload(child_inverse, k, (held,)) for k in range(kids - 1)]
        inverses = [b[0] for b in brought]
        tokens = tuple(b[1] for b in brought)
        beside, across = to_col(held), to_row(held, 2)
        cut = held.shape[0] // 2
        _, near = join([[held, beside]], (1,), tokens, False, 2)
        near_other = [to_row(x, 1) for x in near]
        rest = [to_col(across[:cut]), to_row(beside[cut:], 2)]
        for k in range(kids):
            (picked[k],) = gather(
                [near, near_other], [0, 1], maps, slot_rows, k, row_1, order, None, None, (across,)
            )
        _, far = join([[across, *rest]], (1,), tuple(picked), False)
        far_other = [to_row(x, 1) for x in far]
        root_solution, token = reorder(near, order)
        last_blocks, last_at = [far, far_other], [2, 3]
    else:
        (part,) = part
        panels += [preload(child_panel, k, (part,))[0] for k in range(1, kids)]
        inverses = [preload(child_inverse, k, (part,))[0] for k in range(kids - 1)]
        for bit in bits(cols):
            part = add(part, to_col(part, bit)).astype(BF16)
        own = jnp.zeros((case_count, root_rows), BF16)
        for j in range(leafs):
            got = part if j == 0 else to_leaf(part, j)
            own = lax.dynamic_update_slice_in_dim(
                own, got, lax.bitwise_xor(leaf, j) * (case_count // leafs), 0
            )
        root_solution = own.astype(F32)
        groups = [own]
        for bit in [1, *bits(rows)[1:]]:
            got = to_row(jnp.stack(groups), bit)
            groups += [got[i] for i in range(len(groups))]
        last_blocks, last_at = [[g] for g in groups], list(range(rows))

    begun = []
    after = ()
    for k in range(kids):
        bring = (child_inverse, k) if k == kids - 1 else None
        full, *brought = gather(
            last_blocks, last_at, maps, slot_rows, k, row_1, order, picked[k], bring, after
        )
        inverses += brought
        sent = held_nn([full], panels[k], core, 1, pieces_of(k))
        kept = held_nn([full], panels[k], core, 0, 1, sent[:1])
        begun.append(core_sum(kept[0], sent))
        after = begun[k][1:]
    solved = first = None
    chunks = 2 if slot_rows % 256 == 0 else 1
    after = (token, *after)
    for k in range(kids):
        _, rounded = row_end(*begun[k], after, forward[k], False, pieces_of(1))
        pair = halves(rounded)
        after = ()
        for at in range(chunks):
            ready = (first,) if k and at else ()
            (out,) = held_nt(*pair, inverses[k], core, at, chunks, after=ready)
            after += (out,)
            terms = [out, to_col(out)]
            for bit in bits(cols)[1:]:
                out = add(*terms).astype(BF16)
                terms = [out, to_col(out, bit)]
            solved, done = finish(solved, kids, k, at, chunks, terms)
            first = done if first is None else first
    return (solved, root_solution)


def solution(mesh):
    sizes = tuple(mesh.shape[a] for a in ("leaf", "row", "col"))
    in_specs = (
        P("leaf", None, "row"),
        P("leaf", "row", "col"),
        P("leaf", "row", "col"),
        P("leaf", None),
        P(None, "row"),
        P("row", "col"),
    )
    out_specs = (P("leaf", None, "row"), P(None, "row"))
    return jax.shard_map(
        functools.partial(on_device, sizes),
        mesh=mesh,
        in_specs=in_specs,
        out_specs=out_specs,
        check_vma=False,
    )
```

```python
import functools

import jax
import jax.numpy as jnp
from jax import lax
from jax.experimental import pallas as pl
from jax.experimental.pallas import tpu as pltpu
from jax.sharding import PartitionSpec as P

BF16 = jnp.bfloat16
F32 = jnp.float32
I16 = jnp.int16
NN = (((1,), (0,)), ((), ()))
NT = (((1,), (1,)), ((), ()))
LANES = 128
ANY = pl.BlockSpec(memory_space=pl.ANY)
WHOLE = pl.BlockSpec(memory_space=pltpu.VMEM)
SCALARS = pl.BlockSpec(memory_space=pltpu.SMEM)
IN_HBM = pl.BlockSpec(memory_space=pltpu.HBM)


def tile_of(extent, *sizes):
    for size in sizes:
        if extent % size == 0:
            return size
    return extent


def params():
    return pltpu.CompilerParams(vmem_limit_bytes=10 * 1024 * 1024)


def cost(flops, nbytes):
    return pl.CostEstimate(flops=flops // 64, bytes_accessed=nbytes // 64, transcendentals=0)


def in_hbm(w):
    return pltpu.with_memory_space_constraint(w, pltpu.HBM)


def in_vmem(w):
    return pltpu.with_memory_space_constraint(w, pltpu.VMEM)


TOKEN = jax.ShapeDtypeStruct((8, LANES), F32)


def preload_kernel(child, w_ref, *rest):
    o_ref, token_ref, sem = rest[-3:]
    copy = pltpu.make_async_copy(w_ref.at[child], o_ref, sem)
    copy.start()
    token_ref[...] = jnp.zeros_like(token_ref)
    copy.wait()


def preload(w, child, after=()):
    return pl.pallas_call(
        functools.partial(preload_kernel, child),
        in_specs=[pl.BlockSpec(memory_space=pltpu.HBM)] + [ANY] * len(after),
        out_specs=[WHOLE, WHOLE],
        out_shape=[pltpu.VMEM(w.shape[1:], w.dtype), TOKEN],
        scratch_shapes=[pltpu.SemaphoreType.DMA],
        compiler_params=params(),
        cost_estimate=cost(0, w[0].size * 2),
    )(in_hbm(w), *after)


def put_pieces(refs, value):
    rows = value.shape[0] // len(refs)
    for i, ref in enumerate(refs):
        ref[...] = value[i * rows : (i + 1) * rows].astype(ref.dtype)


def take_pieces(refs):
    return refs[0][...] if len(refs) == 1 else jnp.concatenate([r[...] for r in refs], axis=0)


def nn_kernel(half_ref, x_ref, w_ref, *outs):
    x = x_ref[0] if len(x_ref.shape) == 3 else x_ref[...]
    product = lax.dot_general(x, w_ref[0], NN, preferred_element_type=F32)
    put_pieces(outs, product)


def nn(x, w, child, core, part, pieces=1, after=()):
    m, k = x.shape[-2:]
    n_half = w.shape[2] // 2
    bn = tile_of(n_half, 768, 512, 384, 256, 128)
    steps = n_half // bn
    if x.ndim == 3:
        x_spec = pl.BlockSpec((1, m, k), lambda i, h: (child, 0, 0))
        x = in_hbm(x)
    else:
        x_spec = pl.BlockSpec((m, k), lambda i, h: (0, 0))

    def kernel(half_ref, x_ref, w_ref, *rest):
        nn_kernel(half_ref, x_ref, w_ref, *rest[len(after) :])

    return pl.pallas_call(
        kernel,
        grid_spec=pltpu.PrefetchScalarGridSpec(
            num_scalar_prefetch=1,
            grid=(steps,),
            in_specs=[
                x_spec,
                pl.BlockSpec(
                    (1, k, bn), lambda i, h: (child, 0, lax.bitwise_xor(h[0], part) * steps + i)
                ),
            ]
            + [ANY] * len(after),
            out_specs=[pl.BlockSpec((m // pieces, bn), lambda i, h: (0, i))] * pieces,
        ),
        out_shape=[jax.ShapeDtypeStruct((m // pieces, n_half), BF16 if part else F32)] * pieces,
        compiler_params=params(),
        cost_estimate=cost(2 * m * k * n_half, 2 * k * n_half),
    )(core, x, in_hbm(w), *after)


def held_nn(x, w, core, part, pieces=1, after=()):
    m, k = sum(p.shape[0] for p in x), x[0].shape[1]
    n_half = w.shape[1] // 2
    bn = tile_of(n_half, 512, 384, 256, 128)

    def kernel(half_ref, *refs):
        x_value, w_ref = take_pieces(refs[: len(x)]), refs[len(x)]
        outs = refs[len(x) + 1 + len(after) :]
        base = lax.bitwise_xor(half_ref[0], part) * n_half
        rows = m // pieces
        for start in range(0, n_half, bn):
            cols = pl.ds(pl.multiple_of(base + start, LANES), bn)
            product = lax.dot_general(x_value, w_ref[:, cols], NN, preferred_element_type=F32)
            for i, out in enumerate(outs):
                out[:, start : start + bn] = product[i * rows : (i + 1) * rows].astype(out.dtype)

    return pl.pallas_call(
        kernel,
        in_specs=[SCALARS] + [WHOLE] * (len(x) + 1) + [ANY] * len(after),
        out_specs=[WHOLE] * pieces,
        out_shape=[jax.ShapeDtypeStruct((m // pieces, n_half), BF16 if part else F32)] * pieces,
        compiler_params=params(),
        cost_estimate=cost(2 * m * k * n_half, 2 * k * n_half),
    )(core, *x, in_vmem(w), *after)


def held_nt(mine, other, w, core, chunk=0, chunks=1, pieces=1, bring=None, after=()):
    m = sum(x.shape[0] for x in mine)
    k_half = mine[0].shape[1]
    u = w.shape[0] // chunks
    bu = tile_of(u, 512, 384, 256, 128)
    first = chunk * u
    extra = [] if bring is None else [in_hbm(bring[0])]

    def kernel(half_ref, *refs):
        at = len(mine) + len(other)
        a, b, w_ref = take_pieces(refs[: len(mine)]), take_pieces(refs[len(mine) : at]), refs[at]
        outs = refs[at + 1 + len(extra) + len(after) :]
        outs, sem = outs[:-1], outs[-1]
        if extra:
            brought = pltpu.make_async_copy(refs[at + 1].at[bring[1]], outs[-1], sem)
            brought.start()
            outs = outs[:-1]
        low = half_ref[0] == 0
        left, right = jnp.where(low, a, b), jnp.where(low, b, a)
        rows = m // pieces
        for start in range(0, u, bu):
            at = slice(first + start, first + start + bu)
            total = lax.dot_general(left, w_ref[at, :k_half], NT, preferred_element_type=F32)
            total += lax.dot_general(right, w_ref[at, k_half:], NT, preferred_element_type=F32)
            for i, out in enumerate(outs):
                out[:, start : start + bu] = total[i * rows : (i + 1) * rows].astype(out.dtype)
        if extra:
            brought.wait()

    shapes = [jax.ShapeDtypeStruct((m // pieces, u), BF16)] * pieces
    if extra:
        shapes.append(pltpu.VMEM(bring[0].shape[1:], bring[0].dtype))
    return pl.pallas_call(
        kernel,
        in_specs=[SCALARS]
        + [WHOLE] * (len(mine) + len(other) + 1)
        + [IN_HBM] * len(extra)
        + [ANY] * len(after),
        out_specs=[WHOLE] * len(shapes),
        out_shape=shapes,
        scratch_shapes=[pltpu.SemaphoreType.DMA],
        compiler_params=params(),
        cost_estimate=cost(4 * m * k_half * u, 4 * k_half * u),
    )(core, *mine, *other, in_vmem(w), *extra, *after)


def spread_kernel(row_ref, map_ref, *rest):
    o_ref = rest[-1]
    u = map_ref.shape[2]
    step = tile_of(u, LANES)
    for start in range(0, u, step):
        row = map_ref[0, :, start : start + step]
        o_ref[0, start : start + step, :] = jnp.broadcast_to(row, (LANES, step)).T.astype(I16)


def spread(maps, row, u, after=()):
    kids = maps.shape[0]
    return pl.pallas_call(
        spread_kernel,
        grid_spec=pltpu.PrefetchScalarGridSpec(
            num_scalar_prefetch=1,
            grid=(kids,),
            in_specs=[pl.BlockSpec((1, 1, u), lambda k, r: (k, 0, r[0]))] + [ANY] * len(after),
            out_specs=pl.BlockSpec((1, u, LANES), lambda k, r: (k, 0, 0)),
        ),
        out_shape=jax.ShapeDtypeStruct((kids, u, LANES), I16),
        compiler_params=params(),
        cost_estimate=cost(kids * u * LANES, 2 * kids * u * LANES),
    )(row, maps, *after)


def store_in_order(order_ref, chunk, store, value):
    for i in range(value.shape[0] // chunk):
        store(
            pl.ds(pl.multiple_of(lax.bitwise_xor(order_ref[0], i) * chunk, chunk), chunk),
            value[i * chunk : (i + 1) * chunk],
        )


def scatter_kernel(block_rows, tile, odd, chunk, *refs):
    row_ref, order_ref, map_ref, upd_ref, *rest = refs
    o_ref = rest[-1]
    j, t = pl.program_id(0), pl.program_id(1)
    dest = lax.bitwise_xor(row_ref[0], 2 * j + odd)
    first = (dest * block_rows + t * tile).astype(I16)
    local = map_ref[0] - first
    u = local.shape[0]
    sub = tile_of(tile, 256, 128)
    upd = upd_ref[...]
    for start in range(0, tile, sub):
        wide = jnp.concatenate([local] * (sub // LANES), axis=1)
        row_ids = lax.broadcasted_iota(I16, (u, sub), 1) + jnp.int16(start)
        hot = jnp.where(row_ids == wide, BF16(1), BF16(0))
        total = lax.dot_general(upd, hot, NN, preferred_element_type=F32)
        if len(rest) == 2:
            at = slice(start, start + sub)
            before = rest[0]

            def store(ds, value, at=at, before=before):
                o_ref[0, ds, at] = (value + before[0, ds, at].astype(F32)).astype(o_ref.dtype)

        else:
            at = slice(start, start + sub)

            def store(ds, value, at=at):
                o_ref[0, ds, at] = value.astype(o_ref.dtype)

        store_in_order(order_ref, chunk, store, total)


def scatter(upd, spread_maps, child, row, order, rows_count, block_rows, odd, before):
    m, u = upd.shape
    tile = tile_of(block_rows, 768, 512, 384, 256, 128)
    count = rows_count // 2
    chunk = m // order[1]
    block = pl.BlockSpec((1, m, tile), lambda j, t, r, o: (j, 0, t))
    in_specs = [
        pl.BlockSpec((1, u, LANES), lambda j, t, r, o: (child, 0, 0)),
        pl.BlockSpec((m, u), lambda j, t, r, o: (0, 0)),
    ]
    args = [spread_maps, upd]
    if before is not None:
        in_specs.append(block)
        args.append(before)
    return pl.pallas_call(
        functools.partial(scatter_kernel, block_rows, tile, odd, chunk),
        grid_spec=pltpu.PrefetchScalarGridSpec(
            num_scalar_prefetch=2,
            grid=(count, block_rows // tile),
            in_specs=in_specs,
            out_specs=block,
        ),
        out_shape=jax.ShapeDtypeStruct((count, m, block_rows), BF16),
        compiler_params=params(),
        cost_estimate=cost(2 * m * u * count * block_rows, 4 * m * count * block_rows),
    )(row, order[0], *args)


def gather_kernel(block_rows, tile, which, counts, chunk, added, steps, bring, row_ref, order_ref, map_ref, *rest):
    rest, sem = rest[:-1], rest[-1]
    if bring is not None:
        source, target = rest[-3 - bring[1]], rest[-1]
        rest = rest[:-1]
        brought = pltpu.make_async_copy(source.at[bring[0]], target, sem)
        pl.when(pl.program_id(0) == 0)(brought.start)
    o_ref = rest[-1]
    slot_map = map_ref[0]
    total, at = None, 0
    for j, count in zip(which, counts):
        pieces = rest[at : at + count]
        at += count
        first = lax.bitwise_xor(row_ref[0], j) * block_rows
        for start in range(0, block_rows, tile):
            local = (slot_map - (first + start)).astype(I16)
            row_ids = lax.broadcasted_iota(I16, (tile, slot_map.shape[1]), 0)
            hot = jnp.where(row_ids == local, BF16(1), BF16(0))
            block = [p[:, start : start + tile] for p in pieces]
            block = block[0] if count == 1 else jnp.concatenate(block, axis=0)
            term = lax.dot_general(block, hot, NN, preferred_element_type=F32)
            total = term if total is None else total + term

    def store(ds, value):
        if added:
            value = value + rest[at][ds, :].astype(F32)
        o_ref[ds, :] = value.astype(o_ref.dtype)

    store_in_order(order_ref, chunk, store, total)
    if bring is not None:
        pl.when(pl.program_id(0) == steps - 1)(brought.wait)


def gather(blocks, which, maps, u, child, row, order, before, bring=None, after=()):
    m = sum(p.shape[0] for p in blocks[0])
    block_rows = blocks[0][0].shape[1]
    tile = tile_of(block_rows, 512, 384, 256, 128)
    bu = tile_of(u, 512, 384, 256, 128)
    chunk = m // order[1]
    counts = [len(b) for b in blocks]
    steps = u // bu
    in_specs = [pl.BlockSpec((1, 1, bu), lambda i, r, o: (child, 0, r[0] * steps + i))]
    args = [maps]
    for p in (p for b in blocks for p in b):
        in_specs.append(pl.BlockSpec(p.shape, lambda i, r, o: (0, 0)))
        args.append(p)
    out_block = pl.BlockSpec((m, bu), lambda i, r, o: (0, i))
    if before is not None:
        in_specs.append(out_block)
        args.append(before)
    if bring is not None:
        in_specs.append(IN_HBM)
        args.append(in_hbm(bring[0]))
    in_specs += [ANY] * len(after)
    shapes, out_specs = [jax.ShapeDtypeStruct((m, u), BF16)], [out_block]
    if bring is not None:
        shapes.append(pltpu.VMEM(bring[0].shape[1:], bring[0].dtype))
        out_specs.append(WHOLE)
    return pl.pallas_call(
        functools.partial(
            gather_kernel, block_rows,
            tile,
            which,
            counts,
            chunk,
            before is not None,
            steps,
            None if bring is None else (bring[1], len(after)),
        ),
        grid_spec=pltpu.PrefetchScalarGridSpec(
            num_scalar_prefetch=2,
            grid=(steps,),
            in_specs=in_specs,
            out_specs=out_specs,
            scratch_shapes=[pltpu.SemaphoreType.DMA],
        ),
        out_shape=shapes,
        compiler_params=params(),
        cost_estimate=cost(
            2 * m * u * len(blocks) * block_rows, 2 * m * len(blocks) * block_rows
        ),
    )(row, order[0], *args, *after)


def finish(held, kids, child, chunk, chunks, terms):
    m, n = terms[0].shape
    place = pl.BlockSpec((1, m, n), lambda i: (child, 0, chunk))
    whole = pl.BlockSpec((m, n), lambda i: (0, 0))

    def kernel(*refs):
        total = refs[0][...].astype(F32)
        for ref in refs[1 : len(terms)]:
            total += ref[...].astype(F32)
        refs[-2][0] = total
        refs[-1][...] = jnp.zeros_like(refs[-1])

    extra = () if held is None else (in_hbm(held),)
    return pl.pallas_call(
        kernel,
        grid=(1,),
        in_specs=[whole] * len(terms) + [ANY] * len(extra),
        out_specs=[place, pl.BlockSpec(TOKEN.shape, lambda i: (0, 0))],
        out_shape=[pltpu.HBM((kids, m, n * chunks), F32), TOKEN],
        input_output_aliases={len(terms): 0} if extra else {},
        compiler_params=params(),
        cost_estimate=cost(m * n, 8 * m * n),
    )(*terms, *extra)


def reorder(pieces, order):
    m, n = sum(p.shape[0] for p in pieces), pieces[0].shape[1]
    chunk = m // order[1]

    def kernel(order_ref, *refs):
        *inputs, o_ref, token_ref = refs

        def store(ds, value):
            o_ref[ds, :] = value

        store_in_order(order_ref, chunk, store, take_pieces(inputs).astype(F32))
        token_ref[...] = jnp.zeros_like(token_ref)

    return pl.pallas_call(
        kernel,
        in_specs=[SCALARS] + [WHOLE] * len(pieces),
        out_specs=[WHOLE, WHOLE],
        out_shape=[jax.ShapeDtypeStruct((m, n), F32), TOKEN],
        compiler_params=params(),
        cost_estimate=cost(m * n, 6 * m * n),
    )(order[0], *pieces)


def join(terms, signs, after=(), wide=True, narrow=1):
    m = sum(x.shape[0] for x in terms[0])
    n = terms[0][0].shape[1]
    counts = [len(t) for t in terms]

    def kernel(*refs):
        outs = refs[sum(counts) + len(after) :]
        total, at = None, 0
        for count, sign in zip(counts, signs):
            value = take_pieces(refs[at : at + count]).astype(F32)
            at += count
            value = value if sign > 0 else -value
            total = value if total is None else total + value
        if wide:
            outs[0][...] = total
            outs = outs[1:]
        if narrow:
            put_pieces(outs, total)

    shapes = [jax.ShapeDtypeStruct((m, n), F32)] if wide else []
    shapes += [jax.ShapeDtypeStruct((m // narrow, n), BF16)] * narrow if narrow else []
    outs = pl.pallas_call(
        kernel,
        in_specs=[WHOLE] * sum(counts) + [ANY] * len(after),
        out_specs=[WHOLE] * len(shapes),
        out_shape=shapes,
        compiler_params=params(),
        cost_estimate=cost(m * n, 12 * m * n),
    )(*[x for t in terms for x in t], *after)
    return (outs[0] if wide else None), (outs[1:] if wide else outs)


def call_whole(kernel, args, shapes, scalars=(), after=()):
    def body(*refs):
        count = len(scalars) + len(args)
        kernel(*refs[:count], *refs[count + len(after) :])

    return pl.pallas_call(
        body,
        in_specs=[SCALARS] * len(scalars) + [WHOLE] * len(args) + [ANY] * len(after),
        out_specs=[WHOLE] * len(shapes),
        out_shape=[jax.ShapeDtypeStruct(*s) for s in shapes],
        compiler_params=params(),
        cost_estimate=cost(args[0].size, 8 * args[0].size),
    )(*scalars, *args, *after)


def cut_core_sum(kept, got):
    _, m, n = kept.shape
    half, cut = m // 2, n // 2

    def kernel(kept_ref, got_ref, left_ref, left_away, right_ref, right_away):
        for j in range(2):
            left = kept_ref[j, :, :cut].astype(F32) + got_ref[j, :, :cut].astype(F32)
            left_ref[j * half : (j + 1) * half] = left[:half]
            left_away[j * half : (j + 1) * half] = left[half:].astype(BF16)
            right = kept_ref[j, :, cut:].astype(F32) + got_ref[j, :, cut:].astype(F32)
            if j == 0:
                right_ref[...] = right
            else:
                right_away[...] = right.astype(BF16)

    shape = (m, cut)
    return call_whole(
        kernel, (kept, got), [(shape, F32), (shape, BF16), (shape, F32), (shape, BF16)]
    )


def cut_rows(kept, got):
    m, n = kept.shape

    def kernel(kept_ref, got_ref, first, second):
        total = kept_ref[...] + got_ref[...].astype(F32)
        first[...] = total[: m // 2]
        second[...] = total[m // 2 :].astype(BF16)

    return call_whole(kernel, (kept, got), [((m // 2, n), F32), ((m // 2, n), BF16)])


def cut_cases(left, left_got, right, right_got, count):
    m, n = left.shape
    piece = m // count

    def kernel(a, b, c, d, *outs):
        sums = a[...] + b[...].astype(F32), c[...] + d[...].astype(F32)
        for i, out in enumerate(outs):
            for at, total in enumerate(sums):
                rows = total[i * piece : (i + 1) * piece]
                out[:, at * n : (at + 1) * n] = rows.astype(out.dtype)

    shapes = [((piece, 2 * n), BF16 if i else F32) for i in range(count)]
    return call_whole(kernel, (left, left_got, right, right_got), shapes)


def residual_of(loads, first, terms, after):
    piece, n = terms[0].shape

    def kernel(first_ref, loads_ref, *refs):
        rows = pl.ds(pl.multiple_of(first_ref[0] * piece, piece), piece)
        total = refs[0][...].astype(F32)
        for ref in refs[1:-1]:
            total += ref[...].astype(F32)
        refs[-1][...] = (loads_ref[rows, :].astype(F32) - total).astype(BF16)

    return call_whole(kernel, (loads, *terms), [((piece, n), BF16)], (first,), after)[0]


def swap(x, axis, bit, size):
    return lax.ppermute(x, axis, [(i, i ^ bit) for i in range(size)])


def add(x, y):
    return x.astype(F32) + y.astype(F32)


def bits(size):
    return [1 << b for b in range(size.bit_length() - 1)]


def on_device(sizes, child_loads, child_inverse, child_panel, child_map, root_loads, root_inverse):
    leafs, rows, cols = sizes
    kids = child_loads.shape[0]
    case_count, root_rows = root_loads.shape
    leaf, row, col = (lax.axis_index(a).astype(jnp.int32) for a in ("leaf", "row", "col"))
    core = lax.bitwise_and(row, 1)[None]
    row_1 = row[None]
    root_w = root_inverse[None]
    piece = case_count // (leafs * cols)
    wide = rows == 4 and cols == 2 and piece % 16 == 0 and root_rows % 256 == 0

    def to_row(x, bit):
        return swap(x, "row", bit, rows)

    def to_col(x, bit=1):
        return swap(x, "col", bit, cols)

    def to_leaf(x, j):
        return swap(x, "leaf", j, leafs)

    def pieces_of(k, m=case_count):
        return 4 if k and m % 64 == 0 else 1

    def core_sum(kept, sent):
        total, narrow = join([[kept], [to_row(x, 1) for x in sent]], (1, 1))
        return total, narrow[0]

    def row_end(total, narrow, after=(), base=None, wide=True, pieces=1):
        steps = bits(rows)[1:]
        for at, bit in enumerate(steps):
            last = at == len(steps) - 1
            terms, signs = [[total], [to_row(narrow, bit)]], (1, 1)
            if last and base is not None:
                terms, signs = [base, *terms], (1, -1, -1)
            total, out = join(
                terms, signs, after, wide or not last, pieces if last else 1
            )
            narrow = out[0]
        return total, out

    def halves(rounded):
        return rounded, [to_row(x, 1) for x in rounded]

    slot_rows = child_panel.shape[1]
    maps = child_map.reshape(kids, 1, child_map.shape[1])

    share = (col * leafs + leaf)[None]
    order = (share, cols * leafs) if wide else (jnp.zeros((1,), jnp.int32), 1)

    begun = []
    after = ()
    for k in range(kids):
        sent = nn(child_loads, child_inverse, k, core, 1, pieces_of(k) // 2 or 1, after)
        (kept,) = nn(child_loads, child_inverse, k, core, 0, 1, sent[:1])
        begun.append(core_sum(kept, sent))
        after = begun[k][1:]
    spread_maps = spread(maps, row_1, slot_rows, after)
    after = (spread_maps,)
    forward = []
    sent = kept = None
    for k in range(kids):
        after = after if k == 0 else (sent,)
        _, rounded = row_end(*begun[k], after, wide=False, pieces=pieces_of(k == 0) // 2 or 1)
        forward.append(rounded)
        if k == 0:
            panel, _ = preload(child_panel, 0, rounded)
        bring = (child_panel, k + 1) if k < kids - 1 else None
        ready = () if kept is None else (kept,)
        upd, *brought = held_nt(*halves(rounded), panel, core, bring=bring, after=ready)
        panel = brought[0] if brought else None
        sent = scatter(upd, spread_maps, k, row_1, order, rows, root_rows, 1, sent)
        kept = scatter(upd, spread_maps, k, row_1, order, rows, root_rows, 0, kept)

    if wide:
        left, left_away, right, right_away = cut_core_sum(kept, to_row(sent, 1))
        left_got, right_got = to_col(left_away), to_row(right_away, 2)
        left, left_away = cut_rows(left, left_got)
        right, right_away = cut_rows(right, right_got)
        mine, *shares = cut_cases(
            left, to_row(left_away, 2), right, to_col(right_away), leafs
        )
        root_held, token = preload(root_w, 0, shares)
        terms = [mine] + [to_leaf(x, j + 1) for j, x in enumerate(shares)]
        residual = residual_of(root_loads, share, terms, (token,))
        residual = [residual, to_col(residual)]
    else:
        total = add(kept, to_row(sent, 1))
        for bit in bits(rows)[1:]:
            total = add(total[0::2], to_row(total[1::2].astype(BF16), bit))
        total = total[0]
        chunk = case_count // leafs

        def cases_of(x, j):
            return lax.dynamic_slice_in_dim(x, lax.bitwise_xor(leaf, j) * chunk, chunk, 0)

        narrow = total.astype(BF16)
        mine_cases = cases_of(total, 0)
        for j in range(1, leafs):
            mine_cases = add(mine_cases, to_leaf(cases_of(narrow, j), j))
        for bit in bits(cols):
            narrow = mine_cases.astype(BF16)
            mine_cases = add(narrow, to_col(narrow, bit))
        residual = [(cases_of(root_loads, 0).astype(F32) - mine_cases).astype(BF16)]
        root_held, _ = preload(root_w, 0, (kept,))

    sent = held_nn(residual, root_held, core, 1)
    kept = held_nn(residual, root_held, core, 0, 1, sent)
    begun = core_sum(kept[0], sent)
    *panels, token = preload(child_panel, 0, begun[1:])
    _, root_forward = row_end(*begun, (token,), wide=False)
    part = held_nt(*halves(root_forward), root_held, core, pieces=2 if wide else 1)

    picked = [None] * kids
    inverses = []
    if wide:
        _, (part,) = join([[part[0]], [to_col(part[1])]], (1, 1), (), False)
        shares = [part] + [to_leaf(part, j) for j in range(1, leafs)]
        brought = [preload(child_panel, k, (part,)) for k in range(1, kids)]
        panels += [b[0] for b in brought]
        _, (held,) = join([shares], (1,), tuple(b[1] for b in brought), False)
        brought = [preload(child_inverse, k, (held,)) for k in range(kids - 1)]
        inverses = [b[0] for b in brought]
        tokens = tuple(b[1] for b in brought)
        beside, across = to_col(held), to_row(held, 2)
        cut = held.shape[0] // 2
        _, near = join([[held, beside]], (1,), tokens, False, 2)
        near_other = [to_row(x, 1) for x in near]
        rest = [to_col(across[:cut]), to_row(beside[cut:], 2)]
        for k in range(kids):
            (picked[k],) = gather(
                [near, near_other], [0, 1], maps, slot_rows, k, row_1, order, None, None, (across,)
            )
        _, far = join([[across, *rest]], (1,), tuple(picked), False)
        far_other = [to_row(x, 1) for x in far]
        root_solution, token = reorder(near, order)
        last_blocks, last_at = [far, far_other], [2, 3]
    else:
        (part,) = part
        panels += [preload(child_panel, k, (part,))[0] for k in range(1, kids)]
        inverses = [preload(child_inverse, k, (part,))[0] for k in range(kids - 1)]
        for bit in bits(cols):
            part = add(part, to_col(part, bit)).astype(BF16)
        own = jnp.zeros((case_count, root_rows), BF16)
        for j in range(leafs):
            got = part if j == 0 else to_leaf(part, j)
            own = lax.dynamic_update_slice_in_dim(
                own, got, lax.bitwise_xor(leaf, j) * (case_count // leafs), 0
            )
        root_solution = own.astype(F32)
        groups = [own]
        for bit in [1, *bits(rows)[1:]]:
            got = to_row(jnp.stack(groups), bit)
            groups += [got[i] for i in range(len(groups))]
        last_blocks, last_at = [[g] for g in groups], list(range(rows))

    begun = []
    after = ()
    for k in range(kids):
        bring = (child_inverse, k) if k == kids - 1 else None
        full, *brought = gather(
            last_blocks, last_at, maps, slot_rows, k, row_1, order, picked[k], bring, after
        )
        inverses += brought
        sent = held_nn([full], panels[k], core, 1, pieces_of(k))
        kept = held_nn([full], panels[k], core, 0, 1, sent[:1])
        begun.append(core_sum(kept[0], sent))
        after = begun[k][1:]
    solved = first = None
    chunks = 2 if slot_rows % 256 == 0 else 1
    after = (token, *after)
    for k in range(kids):
        _, rounded = row_end(*begun[k], after, forward[k], False, pieces_of(1))
        pair = halves(rounded)
        after = ()
        for at in range(chunks):
            ready = (first,) if k and at else ()
            (out,) = held_nt(*pair, inverses[k], core, at, chunks, after=ready)
            after += (out,)
            terms = [out, to_col(out)]
            for bit in bits(cols)[1:]:
                out = add(*terms).astype(BF16)
                terms = [out, to_col(out, bit)]
            solved, done = finish(solved, kids, k, at, chunks, terms)
            first = done if first is None else first
    return (solved, root_solution)


def solution(mesh):
    sizes = tuple(mesh.shape[a] for a in ("leaf", "row", "col"))
    in_specs = (
        P("leaf", None, "row"),
        P("leaf", "row", "col"),
        P("leaf", "row", "col"),
        P("leaf", None),
        P(None, "row"),
        P("row", "col"),
    )
    out_specs = (P("leaf", None, "row"), P(None, "row"))
    return jax.shard_map(
        functools.partial(on_device, sizes),
        mesh=mesh,
        in_specs=in_specs,
        out_specs=out_specs,
        check_vma=False,
    )
```
